32 devices in a mesh: ep: 16 (over z, y, core), rep: 2 (over x).
Axes of the slice: x: 2, y: 2, z: 4, core: 2. Of those that a mesh axis runs over, the one named last changes fastest.
Arguments:
- tokens: bfloat16 [256, 3584], P('ep', 'rep'), may hold values from -6 to 6
- expert_ids: int32 [256, 8], P('ep'), may hold values from 0 to 15, all different within a row; in each aligned block of 16 rows (0 to 15, 16 to 31, ...) at most 12 rows name the same one
- gate_weights: float32 [256, 8], P('ep'), may hold values from 0.05 to 0.5
- up_weight: bfloat16 [16, 3584, 1024], P('ep', 'rep'), may hold values from -0.09375 to 0.09375
- down_weight: bfloat16 [16, 1024, 3584], P('ep', None, 'rep'), may hold values from -0.1875 to 0.1875
Outputs:
- mixture: bfloat16 [256, 3584], P('ep', 'rep')
The draws below stay inside these ranges and needn't reach their ends.
Inputs may be any that keep to these rules, and one draw needn't show every extreme that they name: `expert_ids`: the 8 experts of a token differ. Within the rows of one device (each aligned block of 16 tokens) no expert is named by more than 12 tokens, a bound that some block reaches.
All inputs are finite; a program needn't handle non-finite values.
Results may differ from the reference program's by a relative error of at most 0.017.
Values may be sent and summed in bfloat16 or wider, within the bound.
No kernel may reach another device: no remote copies, remote signals or barrier semaphores. Data moves between devices by JAX's collectives and lax.ppermute only.
A program may use at most 64 MiB of HBM per device.

```python
import math
import jax
import jax.numpy as jnp
import numpy as np
from jax import lax

D = 3584
FF = 1024
TOP = 8
TOK_EP = 16
EXPERTS = 16
TOKENS = 256
DQ = 1792
CAP = 12
N_EP = 16


def level_of(key, dims, cuts, low, top_value):
    loudness = 1.0
    for axis_at, parts in cuts:
        draws = jax.random.uniform(jax.random.fold_in(jax.random.fold_in(key, 6), axis_at), (parts,), jnp.float32, low / len(cuts), top_value / len(cuts))
        loudness = loudness * jnp.repeat(jnp.exp(draws), dims[axis_at] // parts).reshape((-1,) + (1,) * (len(dims) - 1 - axis_at))
    return loudness


def routed_block(own_key, own, number, rows, number_of, top, bound, skew):
    order = jax.random.permutation(own_key, number_of)
    heavy_load, ordinary = shares(number_of, rows * top, bound, skew, True), shares(number_of, rows * top, bound, skew, False)
    places = jnp.arange(number_of)

    def named(tallies, offset_by):
        used = int((tallies > 0).sum())
        fixed = max(1, used // 4)
        moved = fixed + (places - fixed + offset_by * (used - fixed)) % max(1, number_of - fixed)
        return jnp.zeros((number_of,), jnp.int32).at[order[jnp.where(places < fixed, places, moved)]].set(jnp.asarray(tallies, jnp.int32))

    tallies = jnp.where(number % 4 == 0, named(heavy_load, number // 4), named(ordinary, number - number // 4 - 1))
    mixed = jax.random.permutation(jax.random.fold_in(own, 3), number_of)
    donor, receiver = mixed[0:number_of // 2 * 2:2], mixed[1:number_of // 2 * 2:2]
    room = jnp.minimum(tallies[donor] - 1, bound - tallies[receiver]) // 2
    room = jnp.where((donor == order[0]) | (receiver == order[0]) | (tallies[receiver] == 0), 0, jnp.maximum(room, 0))
    moved = jax.random.randint(jax.random.fold_in(own, 4), (number_of // 2,), 0, 1 << 20) % (room + 1)
    tallies = tallies.at[donor].add(-moved).at[receiver].add(moved)
    members = jnp.searchsorted(jnp.cumsum(tallies), jnp.arange(rows * top), side="right").astype(jnp.int32)
    listing = members.reshape(top, rows).T
    listing = listing[jax.random.permutation(jax.random.fold_in(own, 1), rows)]
    offset_by = jax.random.randint(jax.random.fold_in(own, 2), (rows, 1), 0, top)
    return jnp.take_along_axis(listing, (jnp.arange(top)[None, :] + offset_by) % top, axis=1)


def shares(count, total, most, slope, full):
    portions = [(1 << 20) // math.isqrt(rank ** slope) + 1 for rank in range(1, count + 1)]
    largest = most if full else min(most, max(-(-total // count), total * portions[0] // sum(portions)))
    least = 1 if total - largest >= count - 1 else 0
    given, surplus = [largest] + [least] * (count - 1), total - largest - least * (count - 1)
    while surplus > 0:
        candidates = [i for i in range(1, count) if given[i] < largest] or [i for i in range(1, count) if given[i] < most]
        mass, budget = sum([portions[i] for i in candidates]), surplus
        for i in candidates:
            addition = min(most - given[i], max(1, budget * portions[i] // mass), surplus)
            given[i] = given[i] + addition
            surplus = surplus - addition
    return np.array(given)


def centred(own_key, shape, deviation, reach, pieces=(), kind=jnp.bfloat16):
    result = jax.random.normal(own_key, shape, jnp.float32) * deviation
    if len(pieces) > 0:
        result = level_of(own_key, shape, pieces, -0.22, 0.18) * result
    return jnp.clip(result, min=-reach, max=reach).astype(kind)


def setup_inputs(seed: int = 0) -> dict:
    splits = jax.random.split(jax.random.key(seed), 6)
    tokens = centred(splits[0], (TOKENS, D), 1.0, 6.0, ((0, 16), (1, 2)))
    expert_ids_keys = jax.random.split(jax.random.fold_in(splits[1], 1), TOKENS // TOK_EP)
    expert_ids_turns = jax.random.permutation(jax.random.fold_in(splits[1], 3), TOKENS // TOK_EP)
    expert_ids = jax.vmap(lambda own, number: routed_block(jax.random.fold_in(splits[1], 2), own, number, TOK_EP, EXPERTS, TOP, CAP, 2))(expert_ids_keys, expert_ids_turns).reshape((TOKENS, TOP))
    gate_weights = jnp.clip(0.05 + 0.45 * jax.random.uniform(splits[2], (TOKENS, TOP), jnp.float32) ** level_of(splits[2], (TOKENS, TOP), ((0, 16),), -0.2, 0.2), 0.05, 0.5)
    up_weight = centred(splits[3], (EXPERTS, D, FF), D ** -0.5, 0.09375, ((0, 16), (1, 2)))
    down_weight = centred(splits[4], (EXPERTS, FF, D), FF ** -0.5, 0.1875, ((0, 16), (2, 2)))
    return dict(tokens=tokens, expert_ids=expert_ids, gate_weights=gate_weights, up_weight=up_weight, down_weight=down_weight)


def expert_rows(inputs, up_matrix, down_matrix):
    pre = jnp.zeros((inputs.shape[0], FF), jnp.float32)
    for block in range(D // DQ):
        part = jnp.dot(inputs[:, block * DQ:(block + 1) * DQ], up_matrix[block * DQ:(block + 1) * DQ], preferred_element_type=jnp.float32)
        rounded = lax.optimization_barrier(part.astype(jnp.bfloat16))
        pre = pre + rounded.astype(jnp.float32)
    hidden = jax.nn.silu(pre).astype(jnp.bfloat16)
    return jnp.dot(hidden, down_matrix, preferred_element_type=jnp.float32).astype(jnp.bfloat16)


def reference(tokens, expert_ids, gate_weights, up_weight, down_weight):
    rows_total = TOKENS * TOP
    flat_ids = expert_ids.reshape(-1).astype(jnp.int32)
    order = jnp.argsort(flat_ids, stable=True).astype(jnp.int32)
    matches = (flat_ids[:, None] == jnp.arange(EXPERTS, dtype=jnp.int32)[None, :]).astype(jnp.int32)
    counts = jnp.sum(matches, axis=0).astype(jnp.int32)
    starts = (jnp.cumsum(counts) - counts).astype(jnp.int32)
    limit = N_EP * CAP

    def one_expert(expert):
        offsets = jnp.arange(limit, dtype=jnp.int32)
        positions = starts[expert] + offsets
        valid = offsets < counts[expert]
        row_ids = order[jnp.minimum(positions, rows_total - 1)].astype(jnp.int32)
        inputs = tokens[row_ids // TOP]
        outputs = expert_rows(inputs, up_weight[expert], down_weight[expert])
        target = jnp.where(valid, row_ids, rows_total).astype(jnp.int32)
        return outputs, target

    outputs, targets = lax.map(one_expert, jnp.arange(EXPERTS, dtype=jnp.int32))
    placed = jnp.zeros((rows_total, D), jnp.bfloat16).at[targets.reshape(-1)].set(outputs.reshape(-1, D), mode="drop")
    picked = placed.astype(jnp.float32).reshape(TOKENS, TOP, D)
    return jnp.sum(gate_weights[:, :, None] * picked, axis=1).astype(jnp.bfloat16)
```

```python
import functools

import jax
import jax.numpy as jnp
from jax import lax
from jax.experimental import pallas as pl
from jax.experimental.pallas import tpu as pltpu
from jax.sharding import PartitionSpec as P

LANES = 128
VMEM = pl.BlockSpec(memory_space=pltpu.VMEM)
SMEM = pl.BlockSpec(memory_space=pltpu.SMEM)
F32, BF16 = jnp.float32, jnp.bfloat16


def call(kernel, outs, args, specs=None, scratch=(), limit=None):
    return pl.pallas_call(
        kernel,
        out_shape=outs,
        in_specs=specs or [VMEM] * len(args),
        out_specs=jax.tree.map(lambda _: VMEM, outs),
        scratch_shapes=scratch,
        compiler_params=pltpu.CompilerParams(vmem_limit_bytes=limit),
    )(*args)


def iota(shape, dim):
    return lax.broadcasted_iota(jnp.int32, shape, dim)


def dot(a, b):
    return jnp.dot(a, b, preferred_element_type=F32)


def pack_kernel(tok_ref, ids_ref, gates_ref, out_ref):
    rows, width = tok_ref.shape
    top = ids_ref.shape[0]
    expert = iota((rows, rows), 0)
    gate = jnp.zeros((rows, rows), F32)
    mask = jnp.zeros((rows, rows), F32)
    for k in range(top):
        hit = ids_ref[k : k + 1, :] == expert
        gate = gate + jnp.where(hit, gates_ref[k : k + 1, :], 0.0)
        mask = mask + jnp.where(hit, 1.0, 0.0)
    hi = gate.astype(BF16)
    rest = gate - hi.astype(F32)
    mid = rest.astype(BF16)
    low = (rest - mid.astype(F32)).astype(BF16)
    earlier = (iota((rows, rows), 0) < iota((rows, rows), 1)).astype(BF16)
    rank = (mask * (dot(mask.astype(BF16), earlier) + 1.0)).astype(BF16)
    routing = jnp.zeros((rows, LANES), F32)
    for q, part in enumerate((hi, mid, low, rank)):
        place = (iota((rows, LANES), 0) + q * rows == iota((rows, LANES), 1)).astype(BF16)
        routing = routing + dot(part, place)
    out_ref[:, :width] = tok_ref[...]
    out_ref[:, width:] = routing.astype(BF16)


def spread(routing, q, rows, n):
    total = n * rows
    take = (iota((LANES, total), 0) == q * rows + iota((LANES, total), 1) % rows).astype(BF16)
    every = dot(routing, take)
    return jnp.sum(
        jnp.where(iota((n, total), 1) // rows == iota((n, total), 0), every, 0.0), axis=0, keepdims=True
    )


def selection(routing, rows, cap, n):
    rank = spread(routing, 3, rows, n)
    slot = iota((n * cap, n * rows), 0)
    token = iota((n * cap, n * rows), 1)
    mine = slot // cap == token // rows
    wanted = (slot % cap + 1).astype(F32)
    return jnp.where(mine & (wanted == rank), 1.0, 0.0)


def up_kernel(rows, cap, groups, me_ref, w_ref, *refs):
    pieces = refs[: len(groups)]
    pre_ref, routing_ref, x_ref = refs[len(groups) :]
    width = w_ref.shape[0]
    n = sum(groups)
    here = iota((rows, LANES), 0) == me_ref[0]
    at = 0
    lines = []
    for ref, count in zip(pieces, groups):
        x_ref[at * rows : (at + count) * rows, :] = ref[:, :width]
        for j in range(count):
            block = ref[j * rows : (j + 1) * rows, width:].astype(F32)
            lines.append(jnp.sum(jnp.where(here, block, 0.0), axis=0, keepdims=True))
        at += count
    routing = jnp.concatenate(lines, axis=0).astype(BF16)
    routing_ref[...] = routing
    sel = selection(routing, rows, cap, n).astype(BF16)
    step = 256
    for c in range(0, w_ref.shape[1], step):
        part = dot(x_ref[...], w_ref[:, c : c + step]).astype(BF16)
        pre_ref[:, c : c + step] = dot(sel, part).astype(BF16)


def down_kernel(rows, cap, n, routing_ref, a_ref, b_ref, w_ref, keep_ref, send_ref):
    v = a_ref[...].astype(F32) + b_ref[...].astype(F32)
    hidden = (v / (1.0 + jnp.exp(-v))).astype(BF16)
    routing = routing_ref[...]
    sel = selection(routing, rows, cap, n)
    gate = spread(routing, 0, rows, n) + spread(routing, 1, rows, n) + spread(routing, 2, rows, n)
    gate = jnp.sum(sel * gate, axis=1, keepdims=True)
    sel = sel.astype(BF16)
    half = n * rows // 2
    step = 256
    for c in range(0, w_ref.shape[1], step):
        out = dot(hidden, w_ref[:, c : c + step]).astype(BF16)
        out = (gate * out.astype(F32)).astype(BF16)
        out = lax.dot_general(sel, out, (((0,), (0,)), ((), ())), preferred_element_type=F32).astype(BF16)
        keep_ref[:, c : c + step] = out[:half]
        send_ref[:, c : c + step] = out[half:]


def pairs_kernel(a_ref, b_ref, own_ref, *sends):
    rows = own_ref.shape[0]
    for k, ref in enumerate((own_ref,) + sends):
        at = pl.ds(k * rows, rows)
        ref[...] = (a_ref[at, :].astype(F32) + b_ref[at, :].astype(F32)).astype(ref.dtype)


def half_kernel(rows, own_ref, *refs):
    total = own_ref[...]
    for ref in refs[:-2]:
        total = total + ref[...].astype(F32)
    keep_ref, send_ref = refs[-2:]
    keep_ref[...] = total[:rows]
    send_ref[...] = total[rows:].astype(BF16)


def last_kernel(keep_ref, got_ref, out_ref):
    out_ref[...] = (keep_ref[...] + got_ref[...].astype(F32)).astype(BF16)


def gathered(tokens, expert_ids, gate_weights, up_weight, down_weight, cap):
    n = lax.axis_size("ep")
    rows, width = tokens.shape
    near = n // 4
    shape = jax.ShapeDtypeStruct

    def swap(x, distance):
        return lax.ppermute(x, "ep", [(i, i ^ distance) for i in range(n)])

    packed = call(
        pack_kernel, shape((rows, width + LANES), BF16), (tokens, expert_ids.T, gate_weights.T)
    )
    both = jnp.concatenate([packed, swap(packed, 2 * near)], axis=0)
    blocks = [both] + [swap(both, 2 * k) for k in range(1, near)]
    blocks = blocks + [swap(b, 1) for b in blocks]
    order = [2] * len(blocks)
    me = lax.axis_index("ep").astype(jnp.int32).reshape(1)
    hidden = up_weight.shape[2]
    pre, routing = call(
        functools.partial(up_kernel, rows, cap, order),
        (shape((n * cap, hidden), BF16), shape((n, LANES), BF16)),
        (me, up_weight[0], *blocks),
        specs=[SMEM] + [VMEM] * (1 + len(blocks)),
        scratch=[pltpu.VMEM((n * rows, width), BF16)],
    )
    other = lax.ppermute(pre, "rep", [(0, 1), (1, 0)])
    keep, send = call(
        functools.partial(down_kernel, rows, cap, n),
        (shape((n // 2 * rows, width), BF16),) * 2,
        (routing, pre, other, down_weight[0]),
    )
    got = swap(send, 1)
    own, *sends = call(
        pairs_kernel,
        (shape((2 * rows, width), F32),) + (shape((2 * rows, width), BF16),) * (near - 1),
        (keep, got),
    )
    back = [swap(s, 2 * k) for k, s in enumerate(sends, 1)]
    mine, theirs = call(
        functools.partial(half_kernel, rows),
        (shape((rows, width), F32), shape((rows, width), BF16)),
        (own, *back),
    )
    return call(last_kernel, shape((rows, width), BF16), (mine, swap(theirs, 2 * near)))


def exchanged(tokens, expert_ids, gate_weights, up_weight, down_weight, capacity):
    n_peers = lax.axis_size("ep")
    tok_rows, top_count = expert_ids.shape
    width_part = tokens.shape[1]
    flat_ids = expert_ids.reshape(-1)
    onehot = (flat_ids[:, None] == jnp.arange(n_peers, dtype=jnp.int32)[None, :]).astype(jnp.int32)
    before = jnp.cumsum(onehot, axis=0) - onehot
    ranking = jnp.sum(before * onehot, axis=1)
    slot_index = flat_ids * capacity + ranking
    token_of_row = jnp.arange(tok_rows * top_count, dtype=jnp.int32) // top_count
    outbound = (
        jnp.zeros((n_peers * capacity, width_part), tokens.dtype)
        .at[slot_index]
        .set(tokens[token_of_row])
    )
    inbound = lax.all_to_all(outbound, "ep", split_axis=0, concat_axis=0, tiled=True)
    pre_share = lax.psum_scatter(
        jnp.dot(inbound, up_weight[0], preferred_element_type=F32).astype(BF16),
        "rep",
        scatter_dimension=0,
        tiled=True,
    ).astype(F32)
    hidden_share = jax.nn.silu(pre_share).astype(BF16)
    expert_out = jnp.dot(
        lax.all_gather(hidden_share, "rep", axis=0, tiled=True),
        down_weight[0],
        preferred_element_type=F32,
    ).astype(BF16)
    returned = lax.all_to_all(expert_out, "ep", split_axis=0, concat_axis=0, tiled=True)
    picked = returned[slot_index].astype(F32).reshape(tok_rows, top_count, width_part)
    mixture = jnp.sum(gate_weights[:, :, None] * picked, axis=1)
    return mixture.astype(BF16)


def local(tokens, expert_ids, gate_weights, up_weight, down_weight):
    n = lax.axis_size("ep")
    rows, top = expert_ids.shape
    cap = min(rows, max(2, 3 * rows * top // (2 * n)))
    fits = n <= rows and 4 * rows <= LANES and n >= 8 and n & (n - 1) == 0
    plan = gathered if fits and lax.axis_size("rep") == 2 else exchanged
    return plan(tokens, expert_ids, gate_weights, up_weight, down_weight, cap)


def solution(mesh):
    placed = (
        P("ep", "rep"),
        P("ep", None),
        P("ep", None),
        P("ep", "rep", None),
        P("ep", None, "rep"),
    )
    return jax.shard_map(
        local, mesh=mesh, in_specs=placed, out_specs=P("ep", "rep"), check_vma=False
    )
```

```python
import functools

import jax
import jax.numpy as jnp
from jax import lax
from jax.experimental import pallas as pl
from jax.experimental.pallas import tpu as pltpu
from jax.sharding import PartitionSpec as P

LANES = 128
VMEM = pl.BlockSpec(memory_space=pltpu.VMEM)
HBM = pl.BlockSpec(memory_space=pltpu.HBM)
SMEM = pl.BlockSpec(memory_space=pltpu.SMEM)
F32, BF16 = jnp.float32, jnp.bfloat16


def call(kernel, outs, args, specs=None, scratch=(), limit=8 << 20, after=(), aliases={}):
    specs = specs or [VMEM] * len(args)
    args = [pltpu.with_memory_space_constraint(a, pltpu.HBM) if s is HBM else a for a, s in zip(args, specs)]

    def body(*refs):
        kernel(*refs[: len(args)], *refs[len(args) + len(after) :])

    return pl.pallas_call(
        body,
        out_shape=outs,
        in_specs=specs + [pl.BlockSpec(memory_space=pl.ANY)] * len(after),
        out_specs=jax.tree.map(lambda _: VMEM, outs),
        scratch_shapes=scratch,
        input_output_aliases=aliases,
        cost_estimate=pl.CostEstimate(flops=1, bytes_accessed=1, transcendentals=0),
        compiler_params=pltpu.CompilerParams(vmem_limit_bytes=limit),
    )(*args, *after)


def tie(x, *after):
    return call(lambda x_ref, out_ref: None, jax.ShapeDtypeStruct(x.shape, x.dtype), (x,), after=after, aliases={0: 0})


def iota(shape, dim):
    return lax.broadcasted_iota(jnp.int32, shape, dim)


def dot(a, b):
    return jnp.dot(a, b, preferred_element_type=F32)


def pack_kernel(tok_ref, ids_hbm, gates_hbm, out_ref, ids_ref, gates_ref, sems):
    rows, width = tok_ref.shape
    top = ids_ref.shape[0]
    copies = [
        pltpu.make_async_copy(ids_hbm, ids_ref, sems.at[0]),
        pltpu.make_async_copy(gates_hbm, gates_ref, sems.at[1]),
        pltpu.make_async_copy(tok_ref, out_ref.at[:, :width], sems.at[2]),
    ]
    for copy in copies:
        copy.start()
    copies[0].wait()
    copies[1].wait()
    expert = iota((rows, rows), 0)
    gate = jnp.zeros((rows, rows), F32)
    mask = jnp.zeros((rows, rows), F32)
    for k in range(top):
        hit = ids_ref[k : k + 1, :] == expert
        gate = gate + jnp.where(hit, gates_ref[k : k + 1, :], 0.0)
        mask = mask + jnp.where(hit, 1.0, 0.0)
    hi = gate.astype(BF16)
    rest = gate - hi.astype(F32)
    mid = rest.astype(BF16)
    low = (rest - mid.astype(F32)).astype(BF16)
    earlier = (iota((rows, rows), 0) < iota((rows, rows), 1)).astype(BF16)
    rank = (mask * (dot(mask.astype(BF16), earlier) + 1.0)).astype(BF16)
    routing = jnp.zeros((rows, LANES), F32)
    for q, part in enumerate((hi, mid, low, rank)):
        place = (iota((rows, LANES), 0) + q * rows == iota((rows, LANES), 1)).astype(BF16)
        routing = routing + dot(part, place)
    out_ref[:, width:] = routing.astype(BF16)
    copies[2].wait()


def load_kernel(w_hbm, w_ref, sems):
    parts = sems.shape[0]
    rows = w_ref.shape[0] // parts
    copies = [
        pltpu.make_async_copy(w_hbm.at[pl.ds(i * rows, rows)], w_ref.at[pl.ds(i * rows, rows)], sems.at[i])
        for i in range(parts)
    ]
    for copy in copies:
        copy.start()
    for copy in copies:
        copy.wait()


def join_kernel(a_ref, b_ref, out_ref):
    rows = a_ref.shape[0]
    out_ref[:rows, :] = a_ref[...]
    out_ref[rows:, :] = b_ref[...]


def routed(routing, rows, q):
    n = routing.shape[0]
    first = pltpu.roll(routing, (LANES - q * rows) % LANES, 1) if q else routing
    lined = pltpu.roll(first, 0, 1, stride=rows, stride_axis=0)
    mine = iota((n, LANES), 1) // rows == iota((n, LANES), 0)
    return jnp.sum(jnp.where(mine, lined, 0.0), axis=0, keepdims=True)[:, : n * rows]


def selection(routing, rows, cap):
    n = routing.shape[0]
    rank = routed(routing, rows, 3).astype(jnp.int32)
    at = iota((1, n * rows), 1) // rows * cap + rank - 1
    return iota((n * cap, n * rows), 0) == jnp.where(rank > 0, at, -1)


def up_kernel(rows, cap, w_ref, *refs):
    blocks, (pre_ref, routing_ref, x_ref) = refs[:-3], refs[-3:]
    width = w_ref.shape[0]
    here = iota((rows, LANES), 0) == lax.axis_index("ep")
    lines = []
    for i, ref in enumerate(blocks):
        size = ref.shape[0]
        x_ref[i * size : (i + 1) * size, :] = ref[:, :width]
        for j in range(0, size, rows):
            block = ref[j : j + rows, width:].astype(F32)
            lines.append(jnp.sum(jnp.where(here, block, 0.0), axis=0, keepdims=True))
    routing = jnp.concatenate(lines, axis=0)
    routing_ref[...] = routing
    step = 256
    parts = [dot(x_ref[...], w_ref[:, c : c + step]).astype(BF16) for c in range(0, w_ref.shape[1], step)]
    sel = jnp.where(selection(routing, rows, cap), 1.0, 0.0).astype(BF16)
    for i, part in enumerate(parts):
        pre_ref[:, i * step : (i + 1) * step] = dot(sel, part).astype(BF16)


def plan_kernel(rows, cap, routing_ref, turned_ref, gate_ref):
    routing = routing_ref[...]
    total, slots = turned_ref.shape
    sel = jnp.where(selection(routing, rows, cap), 1.0, 0.0)
    turned_ref[...] = jnp.transpose(sel).astype(BF16)
    gate = routed(routing, rows, 0) + routed(routing, rows, 1) + routed(routing, rows, 2)
    gate_ref[...] = jnp.transpose(jnp.broadcast_to(gate, (LANES, total)))


def down_kernel(turned_ref, gate_ref, a_ref, b_ref, w_ref, keep_ref, send_ref):
    v = a_ref[...].astype(F32) + b_ref[...].astype(F32)
    hidden = (v / (1.0 + jnp.exp(-v))).astype(BF16)
    hidden = dot(turned_ref[...], hidden).astype(BF16)
    half = keep_ref.shape[0]
    step = 256
    for c in range(0, w_ref.shape[1], step):
        out = dot(hidden, w_ref[:, c : c + step]).astype(BF16).astype(F32)
        out = (out * jnp.concatenate([gate_ref[...]] * (step // LANES), axis=1)).astype(BF16)
        keep_ref[:, c : c + step] = out[:half]
        send_ref[:, c : c + step] = out[half:]


def pairs_kernel(a_ref, b_ref, *outs):
    rows = outs[0].shape[0]
    for k, ref in enumerate(outs):
        at = pl.ds(k * rows, rows)
        ref[...] = (a_ref[at, :].astype(F32) + b_ref[at, :].astype(F32)).astype(ref.dtype)


def half_kernel(rows, own_ref, *refs):
    total = own_ref[...]
    for ref in refs[:-2]:
        total = total + ref[...].astype(F32)
    keep_ref, send_ref = refs[-2:]
    keep_ref[...] = total[:rows]
    send_ref[...] = total[rows:].astype(BF16)


def last_kernel(keep_ref, got_ref, out_ref):
    out_ref[...] = (keep_ref[...] + got_ref[...].astype(F32)).astype(BF16)


def gathered(tokens, expert_ids, gate_weights, up_weight, down_weight, cap):
    n = lax.axis_size("ep")
    rows, width = tokens.shape
    near = n // 4
    hidden = up_weight.shape[2]
    shape = jax.ShapeDtypeStruct
    dma = pltpu.SemaphoreType.DMA

    def swap(x, distance):
        return lax.ppermute(x, "ep", [(i, i ^ distance) for i in range(n)])

    def load(weight, *after):
        out = pltpu.VMEM(weight.shape, BF16)
        return call(load_kernel, out, (weight,), specs=[HBM], scratch=[dma((8,))], after=after)

    packed = call(
        pack_kernel,
        shape((rows, width + LANES), BF16),
        (tokens, expert_ids.T, gate_weights.T),
        specs=[HBM] * 3,
        scratch=[pltpu.VMEM(expert_ids.shape[::-1], jnp.int32), pltpu.VMEM(expert_ids.shape[::-1], F32), dma((3,))],
    )
    far = swap(packed, 2 * near)
    up = load(up_weight[0])
    block = call(join_kernel, shape((2 * rows, width + LANES), BF16), (packed, far), after=(up,))
    blocks = [block] + [swap(block, 2 * k) for k in range(1, near)]
    halves = (blocks[: near // 2], blocks[near // 2 :])
    started = []
    for half in halves:
        half = half + [swap(b, 1) for b in half]
        count = 2 * len(half)
        pre, routing = call(
            functools.partial(up_kernel, rows, cap),
            (shape((count * cap, hidden), BF16), shape((count, LANES), F32)),
            (up, *half),
            scratch=[pltpu.VMEM((count * rows, width), BF16)],
        )
        turned, gate = call(
            functools.partial(plan_kernel, rows, cap),
            (shape((count * rows, count * cap), BF16), shape((count * rows, LANES), F32)),
            (routing,),
        )
        started.append((count, turned, gate, pre, lax.ppermute(pre, "rep", [(0, 1), (1, 0)])))
    down = load(down_weight[0], started[-1][3])
    sums = []
    for i, (count, turned, gate, pre, other) in enumerate(started):
        keep, send = call(
            down_kernel,
            (shape((count // 2 * rows, width), BF16),) * 2,
            (turned, gate, pre, other, down),
        )
        sums += call(
            pairs_kernel,
            tuple(
                shape((2 * rows, width), F32 if i == 0 and k == 0 else BF16) for k in range(len(halves[i]))
            ),
            (keep, swap(send, 1)),
        )
    back = [swap(s, 2 * k) for k, s in enumerate(sums) if k > 0]
    mine, theirs = call(
        functools.partial(half_kernel, rows),
        (shape((rows, width), F32), shape((rows, width), BF16)),
        (sums[0], *back),
    )
    return call(last_kernel, shape((rows, width), BF16), (mine, swap(theirs, 2 * near)))


def exchanged(tokens, expert_ids, gate_weights, up_weight, down_weight, capacity):
    n_peers = lax.axis_size("ep")
    tok_rows, top_count = expert_ids.shape
    width_part = tokens.shape[1]
    flat_ids = expert_ids.reshape(-1)
    onehot = (flat_ids[:, None] == jnp.arange(n_peers, dtype=jnp.int32)[None, :]).astype(jnp.int32)
    before = jnp.cumsum(onehot, axis=0) - onehot
    ranking = jnp.sum(before * onehot, axis=1)
    slot_index = flat_ids * capacity + ranking
    token_of_row = jnp.arange(tok_rows * top_count, dtype=jnp.int32) // top_count
    outbound = (
        jnp.zeros((n_peers * capacity, width_part), tokens.dtype)
        .at[slot_index]
        .set(tokens[token_of_row])
    )
    inbound = lax.all_to_all(outbound, "ep", split_axis=0, concat_axis=0, tiled=True)
    pre_share = lax.psum_scatter(
        jnp.dot(inbound, up_weight[0], preferred_element_type=F32).astype(BF16),
        "rep",
        scatter_dimension=0,
        tiled=True,
    ).astype(F32)
    hidden_share = jax.nn.silu(pre_share).astype(BF16)
    expert_out = jnp.dot(
        lax.all_gather(hidden_share, "rep", axis=0, tiled=True),
        down_weight[0],
        preferred_element_type=F32,
    ).astype(BF16)
    returned = lax.all_to_all(expert_out, "ep", split_axis=0, concat_axis=0, tiled=True)
    picked = returned[slot_index].astype(F32).reshape(tok_rows, top_count, width_part)
    mixture = jnp.sum(gate_weights[:, :, None] * picked, axis=1)
    return mixture.astype(BF16)


def local(tokens, expert_ids, gate_weights, up_weight, down_weight):
    n = lax.axis_size("ep")
    rows, top = expert_ids.shape
    cap = min(rows, max(2, 3 * rows * top // (2 * n)))
    fits = n <= rows and 4 * rows <= LANES and n >= 8 and n & (n - 1) == 0
    plan = gathered if fits and lax.axis_size("rep") == 2 else exchanged
    return plan(tokens, expert_ids, gate_weights, up_weight, down_weight, cap)


def solution(mesh):
    placed = (
        P("ep", "rep"),
        P("ep", None),
        P("ep", None),
        P("ep", "rep", None),
        P("ep", None, "rep"),
    )
    return jax.shard_map(
        local, mesh=mesh, in_specs=placed, out_specs=P("ep", "rep"), check_vma=False
    )
```

```python
import functools

import jax
import jax.numpy as jnp
from jax import lax
from jax.experimental import pallas as pl
from jax.experimental.pallas import tpu as pltpu
from jax.sharding import PartitionSpec as P

LANES = 128
VMEM = pl.BlockSpec(memory_space=pltpu.VMEM)
HBM = pl.BlockSpec(memory_space=pltpu.HBM)
SMEM = pl.BlockSpec(memory_space=pltpu.SMEM)
F32, BF16 = jnp.float32, jnp.bfloat16


def call(kernel, outs, args, specs=None, scratch=(), limit=8 << 20, after=(), aliases={}):
    specs = specs or [VMEM] * len(args)
    args = [pltpu.with_memory_space_constraint(a, pltpu.HBM) if s is HBM else a for a, s in zip(args, specs)]

    def body(*refs):
        kernel(*refs[: len(args)], *refs[len(args) + len(after) :])

    return pl.pallas_call(
        body,
        out_shape=outs,
        in_specs=specs + [pl.BlockSpec(memory_space=pl.ANY)] * len(after),
        out_specs=jax.tree.map(lambda _: VMEM, outs),
        scratch_shapes=scratch,
        input_output_aliases=aliases,
        cost_estimate=pl.CostEstimate(flops=1, bytes_accessed=1, transcendentals=0),
        compiler_params=pltpu.CompilerParams(vmem_limit_bytes=limit),
    )(*args, *after)


def tie(x, *after):
    return call(lambda x_ref, out_ref: None, jax.ShapeDtypeStruct(x.shape, x.dtype), (x,), after=after, aliases={0: 0})


def iota(shape, dim):
    return lax.broadcasted_iota(jnp.int32, shape, dim)


def dot(a, b):
    return jnp.dot(a, b, preferred_element_type=F32)


def pack_kernel(tok_ref, ids_hbm, gates_hbm, out_ref, ids_ref, gates_ref, sems):
    rows, width = tok_ref.shape
    top = ids_ref.shape[0]
    copies = [
        pltpu.make_async_copy(ids_hbm, ids_ref, sems.at[0]),
        pltpu.make_async_copy(gates_hbm, gates_ref, sems.at[1]),
        pltpu.make_async_copy(tok_ref, out_ref.at[:, :width], sems.at[2]),
    ]
    for copy in copies:
        copy.start()
    copies[0].wait()
    copies[1].wait()
    expert = iota((rows, rows), 0)
    gate = jnp.zeros((rows, rows), F32)
    mask = jnp.zeros((rows, rows), F32)
    for k in range(top):
        hit = ids_ref[k : k + 1, :] == expert
        gate = gate + jnp.where(hit, gates_ref[k : k + 1, :], 0.0)
        mask = mask + jnp.where(hit, 1.0, 0.0)
    hi = gate.astype(BF16)
    rest = gate - hi.astype(F32)
    mid = rest.astype(BF16)
    low = (rest - mid.astype(F32)).astype(BF16)
    earlier = (iota((rows, rows), 0) < iota((rows, rows), 1)).astype(BF16)
    rank = (mask * (dot(mask.astype(BF16), earlier) + 1.0)).astype(BF16)
    routing = jnp.zeros((rows, LANES), F32)
    for q, part in enumerate((hi, mid, low, rank)):
        place = (iota((rows, LANES), 0) + q * rows == iota((rows, LANES), 1)).astype(BF16)
        routing = routing + dot(part, place)
    out_ref[:, width:] = routing.astype(BF16)
    copies[2].wait()


def load_kernel(w_hbm, w_ref, sems):
    parts = sems.shape[0]
    rows = w_ref.shape[0] // parts
    copies = [
        pltpu.make_async_copy(w_hbm.at[pl.ds(i * rows, rows)], w_ref.at[pl.ds(i * rows, rows)], sems.at[i])
        for i in range(parts)
    ]
    for copy in copies:
        copy.start()
    for copy in copies:
        copy.wait()


def join_kernel(a_ref, b_ref, out_ref):
    rows = a_ref.shape[0]
    out_ref[:rows, :] = a_ref[...]
    out_ref[rows:, :] = b_ref[...]


def routed(routing, rows, q):
    n = routing.shape[0]
    first = pltpu.roll(routing, LANES - q * rows, 1) if q else routing
    lined = pltpu.roll(first, 0, 1, stride=rows, stride_axis=0)
    mine = iota((n, LANES), 1) // rows == iota((n, LANES), 0)
    return jnp.sum(jnp.where(mine, lined, 0.0), axis=0, keepdims=True)


def selection(routing, rows, cap):
    rank = routed(routing, rows, 3).astype(jnp.int32)
    at = iota((1, LANES), 1) // rows * cap + rank - 1
    hit = iota((LANES // rows * cap, LANES), 0) == jnp.where(rank > 0, at, -1)
    return jnp.where(hit, 1.0, 0.0)


def up_kernel(rows, cap, offsets, *refs):
    weights, blocks, (pre_ref, routing_ref, x_ref) = refs[: len(offsets)], refs[len(offsets) : -3], refs[-3:]
    width = weights[0].shape[0]
    pieces = []
    for i, ref in enumerate(blocks):
        size = ref.shape[0]
        x_ref[i * size : (i + 1) * size, :] = ref[:, :width]
        pieces += [ref[j : j + rows, width:].astype(F32) for j in range(0, size, rows)]
    lines = []
    for offset in offsets:
        here = iota((rows, LANES), 0) == lax.axis_index("ep") ^ offset
        lines += [jnp.sum(jnp.where(here, piece, 0.0), axis=0, keepdims=True) for piece in pieces]
    routing = jnp.concatenate(lines + [jnp.zeros_like(lines[0])] * (LANES // rows - len(lines)), axis=0)
    routing_ref[...] = routing
    step = 256
    parts = []
    for c in range(0, weights[0].shape[1], step):
        parts.append([dot(x_ref[...], w_ref[:, c : c + step]).astype(BF16) for w_ref in weights])
    slots, tokens = len(lines) * cap, len(lines) * rows
    sel = selection(routing, rows, cap)[:slots, :tokens].astype(BF16)
    for i, part in enumerate(parts):
        pre_ref[:, i * step : (i + 1) * step] = dot(sel, jnp.concatenate(part, axis=0)).astype(BF16)


def plan_kernel(rows, cap, routing_ref, turned_ref, gate_ref):
    routing = routing_ref[...]
    tokens, slots = turned_ref.shape
    turned_ref[...] = jnp.transpose(selection(routing, rows, cap))[:tokens, :slots].astype(BF16)
    gate = routed(routing, rows, 0) + routed(routing, rows, 1) + routed(routing, rows, 2)
    gate_ref[...] = jnp.transpose(jnp.broadcast_to(gate, (LANES, LANES)))[:tokens]


def down_kernel(experts, terms, turned_ref, gate_ref, a_ref, b_ref, *refs):
    weights, sums, outs = refs[:experts], refs[experts : experts + terms], refs[experts + terms :]
    v = a_ref[...].astype(F32) + b_ref[...].astype(F32)
    hidden = (v / (1.0 + jnp.exp(-v))).astype(BF16)
    hidden = dot(turned_ref[...], hidden).astype(BF16)
    size = hidden.shape[0] // experts
    rows = outs[0].shape[0]
    step = 256
    for c in range(0, weights[0].shape[1], step):
        total = [ref[:, c : c + step] for ref in sums]
        for i, w_ref in enumerate(weights):
            at = slice(i * size, (i + 1) * size)
            out = dot(hidden[at], w_ref[:, c : c + step]).astype(BF16).astype(F32)
            total.append(out * jnp.concatenate([gate_ref[at, :]] * (step // LANES), axis=1))
        total = sum(total[1:], total[0])
        for k, ref in enumerate(outs):
            ref[:, c : c + step] = total[k * rows : (k + 1) * rows].astype(ref.dtype)


def half_kernel(rows, own_ref, *refs):
    total = own_ref[...]
    for ref in refs[:-2]:
        total = total + ref[...].astype(F32)
    keep_ref, send_ref = refs[-2:]
    keep_ref[...] = total[:rows]
    send_ref[...] = total[rows:].astype(BF16)


def last_kernel(keep_ref, got_ref, out_ref):
    out_ref[...] = (keep_ref[...] + got_ref[...].astype(F32)).astype(BF16)


def gathered(tokens, expert_ids, gate_weights, up_weight, down_weight, cap):
    n = lax.axis_size("ep")
    rows, width = tokens.shape
    near = n // 4
    hidden = up_weight.shape[2]
    shape = jax.ShapeDtypeStruct
    dma = pltpu.SemaphoreType.DMA

    def swap(x, distance):
        return lax.ppermute(x, "ep", [(i, i ^ distance) for i in range(n)])

    def load(weight, *after):
        out = pltpu.VMEM(weight.shape, BF16)
        return call(load_kernel, out, (weight,), specs=[HBM], scratch=[dma((8,))], after=after)

    packed = call(
        pack_kernel,
        shape((rows, width + LANES), BF16),
        (tokens, expert_ids.T, gate_weights.T),
        specs=[HBM] * 3,
        scratch=[pltpu.VMEM(expert_ids.shape[::-1], jnp.int32), pltpu.VMEM(expert_ids.shape[::-1], F32), dma((3,))],
    )
    up = load(up_weight[0])
    far = swap(packed, 2 * near)
    block = call(join_kernel, shape((2 * rows, width + LANES), BF16), (packed, far), after=(up,))
    blocks = [block] + [swap(block, 2 * k) for k in range(1, near)]
    down = down_weight[0]
    ups, downs = (up, swap(up_weight[0], 1)), (down, swap(down, 1))

    def raised(offsets, blocks, before=None):
        count, size = len(offsets) * 2 * len(blocks), 2 * len(blocks) * rows
        pre, routing = call(
            functools.partial(up_kernel, rows, cap, offsets),
            (shape((count * cap, hidden), BF16), shape((LANES // rows, LANES), F32)),
            (*(ups[i] for i in offsets), *blocks),
            scratch=[pltpu.VMEM((size, width), BF16)],
        )
        if before is not None:
            pre = tie(pre, before)
        plan = call(
            functools.partial(plan_kernel, rows, cap),
            (shape((count * rows, count * cap), BF16), shape((count * rows, LANES), F32)),
            (routing,),
        )
        return (*plan, pre, lax.ppermute(pre, "rep", [(0, 1), (1, 0)]))

    def lowered(offsets, step, outs, *terms):
        return call(
            functools.partial(down_kernel, len(offsets), len(terms)), outs, (*step, *(downs[i] for i in offsets), *terms)
        )

    pair = shape((2 * rows, width), F32)
    here = raised((0, 1), blocks[:1])
    there = [raised((i,), blocks[1:], here[-1] if i == 0 else None) for i in (0, 1)]
    own = lowered((0, 1), here, pair)
    first = lowered((0,), there[0], shape((2 * (near - 1) * rows, width), F32))
    sends = lowered((1,), there[1], (shape(pair.shape, BF16),) * (near - 1), first)
    back = [swap(s, 2 * k) for k, s in enumerate(sends, 1)]
    mine, theirs = call(
        functools.partial(half_kernel, rows),
        (shape((rows, width), F32), shape((rows, width), BF16)),
        (own, *back),
    )
    return call(last_kernel, shape((rows, width), BF16), (mine, swap(theirs, 2 * near)))


def exchanged(tokens, expert_ids, gate_weights, up_weight, down_weight, capacity):
    n_peers = lax.axis_size("ep")
    tok_rows, top_count = expert_ids.shape
    width_part = tokens.shape[1]
    flat_ids = expert_ids.reshape(-1)
    onehot = (flat_ids[:, None] == jnp.arange(n_peers, dtype=jnp.int32)[None, :]).astype(jnp.int32)
    before = jnp.cumsum(onehot, axis=0) - onehot
    ranking = jnp.sum(before * onehot, axis=1)
    slot_index = flat_ids * capacity + ranking
    token_of_row = jnp.arange(tok_rows * top_count, dtype=jnp.int32) // top_count
    outbound = (
        jnp.zeros((n_peers * capacity, width_part), tokens.dtype)
        .at[slot_index]
        .set(tokens[token_of_row])
    )
    inbound = lax.all_to_all(outbound, "ep", split_axis=0, concat_axis=0, tiled=True)
    pre_share = lax.psum_scatter(
        jnp.dot(inbound, up_weight[0], preferred_element_type=F32).astype(BF16),
        "rep",
        scatter_dimension=0,
        tiled=True,
    ).astype(F32)
    hidden_share = jax.nn.silu(pre_share).astype(BF16)
    expert_out = jnp.dot(
        lax.all_gather(hidden_share, "rep", axis=0, tiled=True),
        down_weight[0],
        preferred_element_type=F32,
    ).astype(BF16)
    returned = lax.all_to_all(expert_out, "ep", split_axis=0, concat_axis=0, tiled=True)
    picked = returned[slot_index].astype(F32).reshape(tok_rows, top_count, width_part)
    mixture = jnp.sum(gate_weights[:, :, None] * picked, axis=1)
    return mixture.astype(BF16)


def local(tokens, expert_ids, gate_weights, up_weight, down_weight):
    n = lax.axis_size("ep")
    rows, top = expert_ids.shape
    cap = min(rows, max(2, 3 * rows * top // (2 * n)))
    fits = n <= rows and 4 * rows <= LANES and n // 2 * rows == LANES and n & (n - 1) == 0
    plan = gathered if fits and lax.axis_size("rep") == 2 else exchanged
    return plan(tokens, expert_ids, gate_weights, up_weight, down_weight, cap)


def solution(mesh):
    placed = (
        P("ep", "rep"),
        P("ep", None),
        P("ep", None),
        P("ep", "rep", None),
        P("ep", None, "rep"),
    )
    return jax.shard_map(
        local, mesh=mesh, in_specs=placed, out_specs=P("ep", "rep"), check_vma=False
    )
```

```python
import functools

import jax
import jax.numpy as jnp
from jax import lax
from jax.experimental import pallas as pl
from jax.experimental.pallas import tpu as pltpu
from jax.sharding import PartitionSpec as P

LANES = 128
VMEM = pl.BlockSpec(memory_space=pltpu.VMEM)
HBM = pl.BlockSpec(memory_space=pltpu.HBM)
SMEM = pl.BlockSpec(memory_space=pltpu.SMEM)
F32, BF16 = jnp.float32, jnp.bfloat16


def call(kernel, outs, args, specs=None, scratch=(), limit=8 << 20, after=(), aliases={}):
    specs = specs or [VMEM] * len(args)
    args = [pltpu.with_memory_space_constraint(a, pltpu.HBM) if s is HBM else a for a, s in zip(args, specs)]

    def body(*refs):
        kernel(*refs[: len(args)], *refs[len(args) + len(after) :])

    return pl.pallas_call(
        body,
        out_shape=outs,
        in_specs=specs + [pl.BlockSpec(memory_space=pl.ANY)] * len(after),
        out_specs=jax.tree.map(lambda _: VMEM, outs),
        scratch_shapes=scratch,
        input_output_aliases=aliases,
        cost_estimate=pl.CostEstimate(flops=1, bytes_accessed=1, transcendentals=0),
        compiler_params=pltpu.CompilerParams(vmem_limit_bytes=limit),
    )(*args, *after)


def tie(x, *after):
    return call(lambda x_ref, out_ref: None, jax.ShapeDtypeStruct(x.shape, x.dtype), (x,), after=after, aliases={0: 0})


def iota(shape, dim):
    return lax.broadcasted_iota(jnp.int32, shape, dim)


def dot(a, b):
    return jnp.dot(a, b, preferred_element_type=F32)


def pack_kernel(tok_ref, ids_hbm, gates_hbm, out_ref, ids_ref, gates_ref, sems):
    rows, width = tok_ref.shape
    top = ids_ref.shape[0]
    copies = [
        pltpu.make_async_copy(ids_hbm, ids_ref, sems.at[0]),
        pltpu.make_async_copy(gates_hbm, gates_ref, sems.at[1]),
        pltpu.make_async_copy(tok_ref, out_ref.at[:, :width], sems.at[2]),
    ]
    for copy in copies:
        copy.start()
    copies[0].wait()
    copies[1].wait()
    expert = iota((rows, rows), 0)
    gate = jnp.zeros((rows, rows), F32)
    mask = jnp.zeros((rows, rows), F32)
    for k in range(top):
        hit = ids_ref[k : k + 1, :] == expert
        gate = gate + jnp.where(hit, gates_ref[k : k + 1, :], 0.0)
        mask = mask + jnp.where(hit, 1.0, 0.0)
    hi = gate.astype(BF16)
    rest = gate - hi.astype(F32)
    mid = rest.astype(BF16)
    low = (rest - mid.astype(F32)).astype(BF16)
    earlier = (iota((rows, rows), 0) < iota((rows, rows), 1)).astype(BF16)
    rank = (mask * (dot(mask.astype(BF16), earlier) + 1.0)).astype(BF16)
    routing = jnp.zeros((rows, LANES), F32)
    for q, part in enumerate((hi, mid, low, rank)):
        place = (iota((rows, LANES), 0) + q * rows == iota((rows, LANES), 1)).astype(BF16)
        routing = routing + dot(part, place)
    out_ref[:, width:] = routing.astype(BF16)
    copies[2].wait()


def load_kernel(w_hbm, w_ref, sems):
    parts = sems.shape[0]
    rows = w_ref.shape[0] // parts
    copies = [
        pltpu.make_async_copy(w_hbm.at[pl.ds(i * rows, rows)], w_ref.at[pl.ds(i * rows, rows)], sems.at[i])
        for i in range(parts)
    ]
    for copy in copies:
        copy.start()
    for copy in copies:
        copy.wait()


def join_kernel(a_ref, b_ref, out_ref):
    rows = a_ref.shape[0]
    out_ref[:rows, :] = a_ref[...]
    out_ref[rows:, :] = b_ref[...]


def routed(routing, rows, q):
    n = routing.shape[0]
    first = pltpu.roll(routing, LANES - q * rows, 1) if q else routing
    lined = pltpu.roll(first, 0, 1, stride=rows, stride_axis=0)
    mine = iota((n, LANES), 1) // rows == iota((n, LANES), 0)
    return jnp.sum(jnp.where(mine, lined, 0.0), axis=0, keepdims=True)


def selection(routing, rows, cap):
    rank = routed(routing, rows, 3).astype(jnp.int32)
    at = iota((1, LANES), 1) // rows * cap + rank - 1
    hit = iota((LANES // rows * cap, LANES), 0) == jnp.where(rank > 0, at, -1)
    return jnp.where(hit, 1.0, 0.0)


def up_kernel(rows, cap, offsets, *refs):
    weights, blocks, (pre_ref, routing_ref, x_ref) = refs[: len(offsets)], refs[len(offsets) : -3], refs[-3:]
    width = weights[0].shape[0]
    pieces = []
    for i, ref in enumerate(blocks):
        size = ref.shape[0]
        x_ref[i * size : (i + 1) * size, :] = ref[:, :width]
        pieces += [ref[j : j + rows, width:].astype(F32) for j in range(0, size, rows)]
    lines = []
    for offset in offsets:
        here = iota((rows, LANES), 0) == lax.axis_index("ep") ^ offset
        lines += [jnp.sum(jnp.where(here, piece, 0.0), axis=0, keepdims=True) for piece in pieces]
    routing = jnp.concatenate(lines + [jnp.zeros_like(lines[0])] * (LANES // rows - len(lines)), axis=0)
    routing_ref[...] = routing
    step = 256
    parts = []
    for c in range(0, weights[0].shape[1], step):
        parts.append([dot(x_ref[...], w_ref[:, c : c + step]).astype(BF16) for w_ref in weights])
    slots, tokens = len(lines) * cap, len(lines) * rows
    sel = selection(routing, rows, cap)[:slots, :tokens].astype(BF16)
    for i, part in enumerate(parts):
        pre_ref[:, i * step : (i + 1) * step] = dot(sel, jnp.concatenate(part, axis=0)).astype(BF16)


def plan_kernel(rows, cap, routing_ref, turned_ref, gate_ref):
    routing = routing_ref[...]
    tokens, slots = turned_ref.shape
    turned_ref[...] = jnp.transpose(selection(routing, rows, cap))[:tokens, :slots].astype(BF16)
    gate = routed(routing, rows, 0) + routed(routing, rows, 1) + routed(routing, rows, 2)
    gate_ref[...] = jnp.transpose(jnp.broadcast_to(gate, (LANES, LANES)))[:tokens]


def down_kernel(experts, terms, turned_ref, gate_ref, a_ref, b_ref, *refs):
    weights, sums, outs = refs[:experts], refs[experts : experts + terms], refs[experts + terms :]
    v = a_ref[...].astype(F32) + b_ref[...].astype(F32)
    hidden = (v / (1.0 + jnp.exp(-v))).astype(BF16)
    hidden = dot(turned_ref[...], hidden).astype(BF16)
    size = hidden.shape[0] // experts
    rows = outs[0].shape[0]
    step = 256
    for c in range(0, weights[0].shape[1], step):
        total = [ref[:, c : c + step] for ref in sums]
        for i, w_ref in enumerate(weights):
            at = slice(i * size, (i + 1) * size)
            out = dot(hidden[at], w_ref[:, c : c + step]).astype(BF16).astype(F32)
            total.append(out * jnp.concatenate([gate_ref[at, :]] * (step // LANES), axis=1))
        total = sum(total[1:], total[0])
        for k, ref in enumerate(outs):
            ref[:, c : c + step] = total[k * rows : (k + 1) * rows].astype(ref.dtype)


def half_kernel(rows, own_ref, *refs):
    total = own_ref[...]
    for ref in refs[:-2]:
        total = total + ref[...].astype(F32)
    keep_ref, send_ref = refs[-2:]
    keep_ref[...] = total[:rows]
    send_ref[...] = total[rows:].astype(BF16)


def last_kernel(keep_ref, got_ref, out_ref):
    out_ref[...] = (keep_ref[...] + got_ref[...].astype(F32)).astype(BF16)


def gathered(tokens, expert_ids, gate_weights, up_weight, down_weight, cap):
    n = lax.axis_size("ep")
    rows, width = tokens.shape
    near = n // 4
    hidden = up_weight.shape[2]
    shape = jax.ShapeDtypeStruct
    dma = pltpu.SemaphoreType.DMA

    def swap(x, distance):
        return lax.ppermute(x, "ep", [(i, i ^ distance) for i in range(n)])

    def load(weight, *after):
        out = pltpu.VMEM(weight.shape, BF16)
        return call(load_kernel, out, (weight,), specs=[HBM], scratch=[dma((8,))], after=after)

    packed = call(
        pack_kernel,
        shape((rows, width + LANES), BF16),
        (tokens, expert_ids.T, gate_weights.T),
        specs=[HBM] * 3,
        scratch=[pltpu.VMEM(expert_ids.shape[::-1], jnp.int32), pltpu.VMEM(expert_ids.shape[::-1], F32), dma((3,))],
    )
    up = load(up_weight[0])
    far = swap(packed, 2 * near)
    block = call(join_kernel, shape((2 * rows, width + LANES), BF16), (packed, far), after=(up,))
    blocks = [block] + [swap(block, 2 * k) for k in range(1, near)]
    down = down_weight[0]
    ups, downs = (up, swap(up_weight[0], 1)), (down, swap(down, 1))

    def raised(offsets, blocks, before=(), after=()):
        count, size = len(offsets) * 2 * len(blocks), 2 * len(blocks) * rows
        pre, routing = call(
            functools.partial(up_kernel, rows, cap, offsets),
            (shape((count * cap, hidden), BF16), shape((LANES // rows, LANES), F32)),
            (*(ups[i] for i in offsets), *blocks),
            scratch=[pltpu.VMEM((size, width), BF16)],
            after=after,
        )
        if before:
            pre = tie(pre, *before)
        plan = call(
            functools.partial(plan_kernel, rows, cap),
            (shape((count * rows, count * cap), BF16), shape((count * rows, LANES), F32)),
            (routing,),
        )
        return (*plan, pre, lax.ppermute(pre, "rep", [(0, 1), (1, 0)]))

    def lowered(offsets, step, outs, *terms, after=()):
        return call(
            functools.partial(down_kernel, len(offsets), len(terms)),
            outs,
            (*step, *(downs[i] for i in offsets), *terms),
            after=after,
        )

    both, single = shape((2 * rows, width), F32), shape((2 * rows, width), BF16)
    here = raised((0, 1), blocks[:1])
    corner = raised((0, 1), blocks[3:])
    there = [raised((i,), blocks[1:3], here[-1:] * (1 - i), corner[2:3] * (1 - i)) for i in (0, 1)]
    diagonal = lowered((0, 1), corner, single)
    first = lowered((0,), there[0], shape((4 * rows, width), F32), after=(diagonal,))
    sends = lowered((1,), there[1], (single,) * 2, first)
    own = lowered((0, 1), here, both, after=sends[:1])
    back = [swap(s, 2 * k) for k, s in enumerate((*sends, diagonal), 1)]
    mine, theirs = call(
        functools.partial(half_kernel, rows),
        (shape((rows, width), F32), shape((rows, width), BF16)),
        (own, *back),
    )
    return call(last_kernel, shape((rows, width), BF16), (mine, swap(theirs, 2 * near)))


def exchanged(tokens, expert_ids, gate_weights, up_weight, down_weight, capacity):
    n_peers = lax.axis_size("ep")
    tok_rows, top_count = expert_ids.shape
    width_part = tokens.shape[1]
    flat_ids = expert_ids.reshape(-1)
    onehot = (flat_ids[:, None] == jnp.arange(n_peers, dtype=jnp.int32)[None, :]).astype(jnp.int32)
    before = jnp.cumsum(onehot, axis=0) - onehot
    ranking = jnp.sum(before * onehot, axis=1)
    slot_index = flat_ids * capacity + ranking
    token_of_row = jnp.arange(tok_rows * top_count, dtype=jnp.int32) // top_count
    outbound = (
        jnp.zeros((n_peers * capacity, width_part), tokens.dtype)
        .at[slot_index]
        .set(tokens[token_of_row])
    )
    inbound = lax.all_to_all(outbound, "ep", split_axis=0, concat_axis=0, tiled=True)
    pre_share = lax.psum_scatter(
        jnp.dot(inbound, up_weight[0], preferred_element_type=F32).astype(BF16),
        "rep",
        scatter_dimension=0,
        tiled=True,
    ).astype(F32)
    hidden_share = jax.nn.silu(pre_share).astype(BF16)
    expert_out = jnp.dot(
        lax.all_gather(hidden_share, "rep", axis=0, tiled=True),
        down_weight[0],
        preferred_element_type=F32,
    ).astype(BF16)
    returned = lax.all_to_all(expert_out, "ep", split_axis=0, concat_axis=0, tiled=True)
    picked = returned[slot_index].astype(F32).reshape(tok_rows, top_count, width_part)
    mixture = jnp.sum(gate_weights[:, :, None] * picked, axis=1)
    return mixture.astype(BF16)


def local(tokens, expert_ids, gate_weights, up_weight, down_weight):
    n = lax.axis_size("ep")
    rows, top = expert_ids.shape
    cap = min(rows, max(2, 3 * rows * top // (2 * n)))
    fits = n <= rows and 4 * rows <= LANES and n // 2 * rows == LANES and n & (n - 1) == 0
    plan = gathered if fits and lax.axis_size("rep") == 2 else exchanged
    return plan(tokens, expert_ids, gate_weights, up_weight, down_weight, cap)


def solution(mesh):
    placed = (
        P("ep", "rep"),
        P("ep", None),
        P("ep", None),
        P("ep", "rep", None),
        P("ep", None, "rep"),
    )
    return jax.shard_map(
        local, mesh=mesh, in_specs=placed, out_specs=P("ep", "rep"), check_vma=False
    )
```

```python
import functools

import jax
import jax.numpy as jnp
from jax import lax
from jax.experimental import pallas as pl
from jax.experimental.pallas import tpu as pltpu
from jax.sharding import PartitionSpec as P

LANES = 128
VMEM = pl.BlockSpec(memory_space=pltpu.VMEM)
HBM = pl.BlockSpec(memory_space=pltpu.HBM)
SMEM = pl.BlockSpec(memory_space=pltpu.SMEM)
F32, BF16 = jnp.float32, jnp.bfloat16


def call(kernel, outs, args, specs=None, scratch=(), limit=8 << 20, after=(), aliases={}):
    specs = specs or [VMEM] * len(args)
    args = [pltpu.with_memory_space_constraint(a, pltpu.HBM) if s is HBM else a for a, s in zip(args, specs)]

    def body(*refs):
        kernel(*refs[: len(args)], *refs[len(args) + len(after) :])

    return pl.pallas_call(
        body,
        out_shape=outs,
        in_specs=specs + [pl.BlockSpec(memory_space=pl.ANY)] * len(after),
        out_specs=jax.tree.map(lambda _: VMEM, outs),
        scratch_shapes=scratch,
        input_output_aliases=aliases,
        cost_estimate=pl.CostEstimate(flops=1, bytes_accessed=1, transcendentals=0),
        compiler_params=pltpu.CompilerParams(vmem_limit_bytes=limit),
    )(*args, *after)


def tie(x, *after):
    return call(lambda x_ref, out_ref: None, jax.ShapeDtypeStruct(x.shape, x.dtype), (x,), after=after, aliases={0: 0})


def iota(shape, dim):
    return lax.broadcasted_iota(jnp.int32, shape, dim)


def dot(a, b):
    return jnp.dot(a, b, preferred_element_type=F32)


def pack_kernel(tok_ref, ids_hbm, gates_hbm, out_ref, ids_ref, gates_ref, sems):
    rows, width = tok_ref.shape
    top = ids_ref.shape[0]
    copies = [
        pltpu.make_async_copy(ids_hbm, ids_ref, sems.at[0]),
        pltpu.make_async_copy(gates_hbm, gates_ref, sems.at[1]),
        pltpu.make_async_copy(tok_ref, out_ref.at[:, :width], sems.at[2]),
    ]
    for copy in copies:
        copy.start()
    copies[0].wait()
    copies[1].wait()
    expert = iota((rows, rows), 0)
    gate = jnp.zeros((rows, rows), F32)
    mask = jnp.zeros((rows, rows), F32)
    for k in range(top):
        hit = ids_ref[k : k + 1, :] == expert
        gate = gate + jnp.where(hit, gates_ref[k : k + 1, :], 0.0)
        mask = mask + jnp.where(hit, 1.0, 0.0)
    hi = gate.astype(BF16)
    rest = gate - hi.astype(F32)
    mid = rest.astype(BF16)
    low = (rest - mid.astype(F32)).astype(BF16)
    earlier = (iota((rows, rows), 0) < iota((rows, rows), 1)).astype(BF16)
    rank = (mask * (dot(mask.astype(BF16), earlier) + 1.0)).astype(BF16)
    routing = jnp.zeros((rows, LANES), F32)
    for q, part in enumerate((hi, mid, low, rank)):
        place = (iota((rows, LANES), 0) + q * rows == iota((rows, LANES), 1)).astype(BF16)
        routing = routing + dot(part, place)
    out_ref[:, width:] = routing.astype(BF16)
    copies[2].wait()


def load_kernel(w_hbm, w_ref, sems):
    parts = sems.shape[0]
    rows = w_ref.shape[0] // parts
    copies = [
        pltpu.make_async_copy(w_hbm.at[pl.ds(i * rows, rows)], w_ref.at[pl.ds(i * rows, rows)], sems.at[i])
        for i in range(parts)
    ]
    for copy in copies:
        copy.start()
    for copy in copies:
        copy.wait()


def join_kernel(a_ref, b_ref, out_ref):
    rows = a_ref.shape[0]
    out_ref[:rows, :] = a_ref[...]
    out_ref[rows:, :] = b_ref[...]


def routed(routing, rows, q):
    n = routing.shape[0]
    first = pltpu.roll(routing, LANES - q * rows, 1) if q else routing
    lined = pltpu.roll(first, 0, 1, stride=rows, stride_axis=0)
    mine = iota((n, LANES), 1) // rows == iota((n, LANES), 0)
    return jnp.sum(jnp.where(mine, lined, 0.0), axis=0, keepdims=True)


def selection(routing, rows, cap):
    rank = routed(routing, rows, 3).astype(jnp.int32)
    at = iota((1, LANES), 1) // rows * cap + rank - 1
    hit = iota((LANES // rows * cap, LANES), 0) == jnp.where(rank > 0, at, -1)
    return jnp.where(hit, 1.0, 0.0)


def up_kernel(rows, cap, offsets, *refs):
    weights, blocks, (pre_ref, routing_ref, x_ref) = refs[: len(offsets)], refs[len(offsets) : -3], refs[-3:]
    width = weights[0].shape[0]
    pieces = []
    for i, ref in enumerate(blocks):
        size = ref.shape[0]
        x_ref[i * size : (i + 1) * size, :] = ref[:, :width]
        pieces += [ref[j : j + rows, width:].astype(F32) for j in range(0, size, rows)]
    tokens = len(pieces) * rows
    x_ref[tokens:, :] = jnp.zeros((LANES - tokens, width), BF16)
    lines = []
    for offset in offsets:
        here = iota((rows, LANES), 0) == lax.axis_index("ep") ^ offset
        lines += [jnp.sum(jnp.where(here, piece, 0.0), axis=0, keepdims=True) for piece in pieces]
    routing = jnp.concatenate(lines + [jnp.zeros_like(lines[0])] * (LANES // rows - len(lines)), axis=0)
    routing_ref[...] = routing
    step = 256
    parts = []
    for c in range(0, weights[0].shape[1], step):
        parts.append([dot(x_ref[...], w_ref[:, c : c + step])[:tokens].astype(BF16) for w_ref in weights])
    sel = selection(routing, rows, cap)[: len(lines) * cap, : len(lines) * rows].astype(BF16)
    for i, part in enumerate(parts):
        pre_ref[:, i * step : (i + 1) * step] = dot(sel, jnp.concatenate(part, axis=0)).astype(BF16)


def plan_kernel(rows, cap, routing_ref, turned_ref, gate_ref):
    routing = routing_ref[...]
    tokens, slots = turned_ref.shape
    turned_ref[...] = jnp.transpose(selection(routing, rows, cap))[:tokens, :slots].astype(BF16)
    gate = routed(routing, rows, 0) + routed(routing, rows, 1) + routed(routing, rows, 2)
    gate_ref[...] = jnp.transpose(jnp.broadcast_to(gate, (LANES, LANES)))[:tokens]


def down_kernel(experts, terms, turned_ref, gate_ref, a_ref, b_ref, *refs):
    weights, sums, outs = refs[:experts], refs[experts : experts + terms], refs[experts + terms :]
    v = a_ref[...].astype(F32) + b_ref[...].astype(F32)
    hidden = (v / (1.0 + jnp.exp(-v))).astype(BF16)
    hidden = dot(turned_ref[...], hidden).astype(BF16)
    size = hidden.shape[0] // experts
    rows = outs[0].shape[0]
    step = 256
    for c in range(0, weights[0].shape[1], step):
        total = [ref[:, c : c + step].astype(F32) for ref in sums]
        for i, w_ref in enumerate(weights):
            at = slice(i * size, (i + 1) * size)
            out = dot(hidden[at], w_ref[:, c : c + step]).astype(BF16).astype(F32)
            total.append(out * jnp.concatenate([gate_ref[at, :]] * (step // LANES), axis=1))
        total = sum(total[1:], total[0])
        for k, ref in enumerate(outs):
            ref[:, c : c + step] = total[k * rows : (k + 1) * rows].astype(ref.dtype)


def half_kernel(rows, own_ref, *refs):
    total = own_ref[...]
    for ref in refs[:-2]:
        total = total + ref[...].astype(F32)
    keep_ref, send_ref = refs[-2:]
    keep_ref[...] = total[:rows]
    send_ref[...] = total[rows:].astype(BF16)


def last_kernel(keep_ref, got_ref, out_ref):
    out_ref[...] = (keep_ref[...] + got_ref[...].astype(F32)).astype(BF16)


def gathered(tokens, expert_ids, gate_weights, up_weight, down_weight, cap):
    n = lax.axis_size("ep")
    rows, width = tokens.shape
    near = n // 4
    hidden = up_weight.shape[2]
    shape = jax.ShapeDtypeStruct
    dma = pltpu.SemaphoreType.DMA

    def swap(x, distance):
        return lax.ppermute(x, "ep", [(i, i ^ distance) for i in range(n)])

    def load(weight, *after):
        out = pltpu.VMEM(weight.shape, BF16)
        return call(load_kernel, out, (weight,), specs=[HBM], scratch=[dma((8,))], after=after)

    packed = call(
        pack_kernel,
        shape((rows, width + LANES), BF16),
        (tokens, expert_ids.T, gate_weights.T),
        specs=[HBM] * 3,
        scratch=[pltpu.VMEM(expert_ids.shape[::-1], jnp.int32), pltpu.VMEM(expert_ids.shape[::-1], F32), dma((3,))],
    )
    up = load(up_weight[0])
    far = swap(packed, 2 * near)
    block = call(join_kernel, shape((2 * rows, width + LANES), BF16), (packed, far), after=(up,))
    blocks = [block] + [swap(block, 2 * k) for k in range(1, near)]
    down = down_weight[0]
    ups, downs = (up, swap(up_weight[0], 1)), (down, swap(down, 1))

    def raised(offsets, blocks, before=(), after=()):
        count = len(offsets) * 2 * len(blocks)
        pre, routing = call(
            functools.partial(up_kernel, rows, cap, offsets),
            (shape((count * cap, hidden), BF16), shape((LANES // rows, LANES), F32)),
            (*(ups[i] for i in offsets), *blocks),
            scratch=[pltpu.VMEM((LANES, width), BF16)],
            after=after,
        )
        if before:
            pre = tie(pre, *before)
        plan = call(
            functools.partial(plan_kernel, rows, cap),
            (shape((count * rows, count * cap), BF16), shape((count * rows, LANES), F32)),
            (routing,),
        )
        return (*plan, pre, lax.ppermute(pre, "rep", [(0, 1), (1, 0)]))

    def lowered(offsets, step, outs, *terms, after=()):
        return call(
            functools.partial(down_kernel, len(offsets), len(terms)),
            outs,
            (*step, *(downs[i] for i in offsets), *terms),
            after=after,
        )

    both, single = shape((2 * rows, width), F32), shape((2 * rows, width), BF16)
    here = raised((0, 1), blocks[:1])
    corner = raised((0, 1), blocks[3:], (), here[:2])
    there = [raised((i,), blocks[1:3], here[-1:] * (1 - i), corner[:3] * (1 - i)) for i in (0, 1)]
    diagonal = lowered((0, 1), corner, single)
    first = lowered((0,), there[0], shape((4 * rows, width), F32), after=(diagonal,))
    sends = lowered((1,), there[1], (single,) * 2, first)
    own = lowered((0, 1), here, both, swap(diagonal, 6), after=sends[:1])
    back = [swap(s, 2 * k) for k, s in enumerate(sends, 1)]
    mine, theirs = call(
        functools.partial(half_kernel, rows),
        (shape((rows, width), F32), shape((rows, width), BF16)),
        (own, *back),
    )
    return call(last_kernel, shape((rows, width), BF16), (mine, swap(theirs, 2 * near)))


def exchanged(tokens, expert_ids, gate_weights, up_weight, down_weight, capacity):
    n_peers = lax.axis_size("ep")
    tok_rows, top_count = expert_ids.shape
    width_part = tokens.shape[1]
    flat_ids = expert_ids.reshape(-1)
    onehot = (flat_ids[:, None] == jnp.arange(n_peers, dtype=jnp.int32)[None, :]).astype(jnp.int32)
    before = jnp.cumsum(onehot, axis=0) - onehot
    ranking = jnp.sum(before * onehot, axis=1)
    slot_index = flat_ids * capacity + ranking
    token_of_row = jnp.arange(tok_rows * top_count, dtype=jnp.int32) // top_count
    outbound = (
        jnp.zeros((n_peers * capacity, width_part), tokens.dtype)
        .at[slot_index]
        .set(tokens[token_of_row])
    )
    inbound = lax.all_to_all(outbound, "ep", split_axis=0, concat_axis=0, tiled=True)
    pre_share = lax.psum_scatter(
        jnp.dot(inbound, up_weight[0], preferred_element_type=F32).astype(BF16),
        "rep",
        scatter_dimension=0,
        tiled=True,
    ).astype(F32)
    hidden_share = jax.nn.silu(pre_share).astype(BF16)
    expert_out = jnp.dot(
        lax.all_gather(hidden_share, "rep", axis=0, tiled=True),
        down_weight[0],
        preferred_element_type=F32,
    ).astype(BF16)
    returned = lax.all_to_all(expert_out, "ep", split_axis=0, concat_axis=0, tiled=True)
    picked = returned[slot_index].astype(F32).reshape(tok_rows, top_count, width_part)
    mixture = jnp.sum(gate_weights[:, :, None] * picked, axis=1)
    return mixture.astype(BF16)


def local(tokens, expert_ids, gate_weights, up_weight, down_weight):
    n = lax.axis_size("ep")
    rows, top = expert_ids.shape
    cap = min(rows, max(2, 3 * rows * top // (2 * n)))
    fits = n <= rows and 4 * rows <= LANES and n // 2 * rows == LANES and n & (n - 1) == 0
    plan = gathered if fits and lax.axis_size("rep") == 2 else exchanged
    return plan(tokens, expert_ids, gate_weights, up_weight, down_weight, cap)


def solution(mesh):
    placed = (
        P("ep", "rep"),
        P("ep", None),
        P("ep", None),
        P("ep", "rep", None),
        P("ep", None, "rep"),
    )
    return jax.shard_map(
        local, mesh=mesh, in_specs=placed, out_specs=P("ep", "rep"), check_vma=False
    )
```

```python
import functools

import jax
import jax.numpy as jnp
from jax import lax
from jax.experimental import pallas as pl
from jax.experimental.pallas import tpu as pltpu
from jax.sharding import PartitionSpec as P

LANES = 128
VMEM = pl.BlockSpec(memory_space=pltpu.VMEM)
HBM = pl.BlockSpec(memory_space=pltpu.HBM)
SMEM = pl.BlockSpec(memory_space=pltpu.SMEM)
F32, BF16 = jnp.float32, jnp.bfloat16


def call(kernel, outs, args, specs=None, scratch=(), limit=8 << 20, after=(), aliases={}):
    specs = specs or [VMEM] * len(args)
    args = [pltpu.with_memory_space_constraint(a, pltpu.HBM) if s is HBM else a for a, s in zip(args, specs)]

    def body(*refs):
        kernel(*refs[: len(args)], *refs[len(args) + len(after) :])

    return pl.pallas_call(
        body,
        out_shape=outs,
        in_specs=specs + [pl.BlockSpec(memory_space=pl.ANY)] * len(after),
        out_specs=jax.tree.map(lambda _: VMEM, outs),
        scratch_shapes=scratch,
        input_output_aliases=aliases,
        cost_estimate=pl.CostEstimate(flops=1, bytes_accessed=1, transcendentals=0),
        compiler_params=pltpu.CompilerParams(vmem_limit_bytes=limit),
    )(*args, *after)


def tie(x, *after):
    return call(lambda x_ref, out_ref: None, jax.ShapeDtypeStruct(x.shape, x.dtype), (x,), after=after, aliases={0: 0})


def iota(shape, dim):
    return lax.broadcasted_iota(jnp.int32, shape, dim)


def dot(a, b):
    return jnp.dot(a, b, preferred_element_type=F32)


def pack_kernel(tok_ref, ids_hbm, gates_hbm, out_ref, ids_ref, gates_ref, sems):
    rows, width = tok_ref.shape
    top = ids_ref.shape[0]
    copies = [
        pltpu.make_async_copy(ids_hbm, ids_ref, sems.at[0]),
        pltpu.make_async_copy(gates_hbm, gates_ref, sems.at[1]),
        pltpu.make_async_copy(tok_ref, out_ref.at[:, :width], sems.at[2]),
    ]
    for copy in copies:
        copy.start()
    copies[0].wait()
    copies[1].wait()
    expert = iota((rows, rows), 0)
    gate = jnp.zeros((rows, rows), F32)
    mask = jnp.zeros((rows, rows), F32)
    for k in range(top):
        hit = ids_ref[k : k + 1, :] == expert
        gate = gate + jnp.where(hit, gates_ref[k : k + 1, :], 0.0)
        mask = mask + jnp.where(hit, 1.0, 0.0)
    hi = gate.astype(BF16)
    rest = gate - hi.astype(F32)
    mid = rest.astype(BF16)
    low = (rest - mid.astype(F32)).astype(BF16)
    earlier = (iota((rows, rows), 0) < iota((rows, rows), 1)).astype(BF16)
    rank = (mask * (dot(mask.astype(BF16), earlier) + 1.0)).astype(BF16)
    routing = jnp.zeros((rows, LANES), F32)
    for q, part in enumerate((hi, mid, low, rank)):
        place = (iota((rows, LANES), 0) + q * rows == iota((rows, LANES), 1)).astype(BF16)
        routing = routing + dot(part, place)
    out_ref[:, width:] = routing.astype(BF16)
    copies[2].wait()


def load_kernel(w_hbm, w_ref, sems):
    parts = sems.shape[0]
    rows = w_ref.shape[0] // parts
    copies = [
        pltpu.make_async_copy(w_hbm.at[pl.ds(i * rows, rows)], w_ref.at[pl.ds(i * rows, rows)], sems.at[i])
        for i in range(parts)
    ]
    for copy in copies:
        copy.start()
    for copy in copies:
        copy.wait()


def join_kernel(a_ref, b_ref, out_ref):
    rows = a_ref.shape[0]
    out_ref[:rows, :] = a_ref[...]
    out_ref[rows:, :] = b_ref[...]


def routed(routing, rows, q):
    n = routing.shape[0]
    first = pltpu.roll(routing, LANES - q * rows, 1) if q else routing
    lined = pltpu.roll(first, 0, 1, stride=rows, stride_axis=0)
    mine = iota((n, LANES), 1) // rows == iota((n, LANES), 0)
    return jnp.sum(jnp.where(mine, lined, 0.0), axis=0, keepdims=True)


def slot_of(routing, rows, cap):
    rank = routed(routing, rows, 3).astype(jnp.int32)
    return jnp.where(rank > 0, iota((1, LANES), 1) // rows * cap + rank - 1, -1)


def selection(routing, rows, cap):
    hit = iota((LANES // rows * cap, LANES), 0) == slot_of(routing, rows, cap)
    return jnp.where(hit, 1.0, 0.0)


def up_kernel(rows, cap, offsets, *refs):
    weights, blocks, (pre_ref, routing_ref, x_ref) = refs[: len(offsets)], refs[len(offsets) : -3], refs[-3:]
    width = weights[0].shape[0]
    pieces = []
    for i, ref in enumerate(blocks):
        size = ref.shape[0]
        x_ref[i * size : (i + 1) * size, :] = ref[:, :width]
        pieces += [ref[j : j + rows, width:].astype(F32) for j in range(0, size, rows)]
    tokens = len(pieces) * rows
    x_ref[tokens:, :] = jnp.zeros((LANES - tokens, width), BF16)
    lines = []
    for offset in offsets:
        here = iota((rows, LANES), 0) == lax.axis_index("ep") ^ offset
        lines += [jnp.sum(jnp.where(here, piece, 0.0), axis=0, keepdims=True) for piece in pieces]
    routing = jnp.concatenate(lines + [jnp.zeros_like(lines[0])] * (LANES // rows - len(lines)), axis=0)
    routing_ref[...] = routing
    step = 256
    parts = []
    for c in range(0, weights[0].shape[1], step):
        parts.append([dot(x_ref[...], w_ref[:, c : c + step])[:tokens].astype(BF16) for w_ref in weights])
    sel = selection(routing, rows, cap)[: len(lines) * cap, : len(lines) * rows].astype(BF16)
    for i, part in enumerate(parts):
        pre_ref[:, i * step : (i + 1) * step] = dot(sel, jnp.concatenate(part, axis=0)).astype(BF16)


def plan_kernel(rows, cap, *refs):
    count = len(refs) // 3
    for routing_ref, turned_ref, gate_ref in zip(refs[:count], refs[count::2], refs[count + 1 :: 2]):
        routing = routing_ref[...]
        tokens, slots = turned_ref.shape
        turned_ref[...] = jnp.transpose(selection(routing, rows, cap))[:tokens, :slots].astype(BF16)
        gate = routed(routing, rows, 0) + routed(routing, rows, 1) + routed(routing, rows, 2)
        gate_ref[...] = jnp.transpose(jnp.broadcast_to(gate, (LANES, LANES)))[:tokens]


def down_kernel(experts, terms, turned_ref, gate_ref, a_ref, b_ref, *refs):
    weights, sums, outs = refs[:experts], refs[experts : experts + terms], refs[experts + terms :]
    v = a_ref[...].astype(F32) + b_ref[...].astype(F32)
    hidden = (v / (1.0 + jnp.exp(-v))).astype(BF16)
    hidden = dot(turned_ref[...], hidden).astype(BF16)
    size = hidden.shape[0] // experts
    rows = outs[0].shape[0]
    step = 256
    for c in range(0, weights[0].shape[1], step):
        total = [ref[:, c : c + step].astype(F32) for ref in sums]
        for i, w_ref in enumerate(weights):
            at = slice(i * size, (i + 1) * size)
            out = dot(hidden[at], w_ref[:, c : c + step]).astype(BF16).astype(F32)
            total.append(out * jnp.concatenate([gate_ref[at, :]] * (step // LANES), axis=1))
        total = sum(total[1:], total[0])
        for k, ref in enumerate(outs):
            ref[:, c : c + step] = total[k * rows : (k + 1) * rows].astype(ref.dtype)


def half_kernel(rows, own_ref, *refs):
    total = own_ref[...]
    for ref in refs[:-2]:
        total = total + ref[...].astype(F32)
    keep_ref, send_ref = refs[-2:]
    keep_ref[...] = total[:rows]
    send_ref[...] = total[rows:].astype(BF16)


def last_kernel(keep_ref, got_ref, out_ref):
    out_ref[...] = (keep_ref[...] + got_ref[...].astype(F32)).astype(BF16)


def gathered(tokens, expert_ids, gate_weights, up_weight, down_weight, cap):
    n = lax.axis_size("ep")
    rows, width = tokens.shape
    near = n // 4
    hidden = up_weight.shape[2]
    shape = jax.ShapeDtypeStruct
    dma = pltpu.SemaphoreType.DMA

    def swap(x, distance):
        return lax.ppermute(x, "ep", [(i, i ^ distance) for i in range(n)])

    def load(weight, *after):
        out = pltpu.VMEM(weight.shape, BF16)
        return call(load_kernel, out, (weight,), specs=[HBM], scratch=[dma((8,))], after=after)

    packed = call(
        pack_kernel,
        shape((rows, width + LANES), BF16),
        (tokens, expert_ids.T, gate_weights.T),
        specs=[HBM] * 3,
        scratch=[pltpu.VMEM(expert_ids.shape[::-1], jnp.int32), pltpu.VMEM(expert_ids.shape[::-1], F32), dma((3,))],
    )
    up = load(up_weight[0])
    far = swap(packed, 2 * near)
    block = call(join_kernel, shape((2 * rows, width + LANES), BF16), (packed, far), after=(up,))
    blocks = [block] + [swap(block, 2 * k) for k in range(1, near)]
    down = down_weight[0]
    ups, downs = (up, swap(up_weight[0], 1)), (down, swap(down, 1))

    def raised(offsets, blocks, before=(), after=()):
        count = len(offsets) * 2 * len(blocks)
        pre, routing = call(
            functools.partial(up_kernel, rows, cap, offsets),
            (shape((count * cap, hidden), BF16), shape((LANES // rows, LANES), F32)),
            (*(ups[i] for i in offsets), *blocks),
            scratch=[pltpu.VMEM((LANES, width), BF16)],
            after=after,
        )
        if before:
            pre = tie(pre, *before)
        return count, routing, pre, lax.ppermute(pre, "rep", [(0, 1), (1, 0)])

    def planned(*steps):
        outs = []
        for count, *_ in steps:
            outs += [shape((count * rows, count * cap), BF16), shape((count * rows, LANES), F32)]
        made = call(functools.partial(plan_kernel, rows, cap), tuple(outs), tuple(step[1] for step in steps))
        return [(*made[2 * i : 2 * i + 2], *step[2:]) for i, step in enumerate(steps)]

    def lowered(offsets, step, outs, *terms, after=()):
        return call(
            functools.partial(down_kernel, len(offsets), len(terms)),
            outs,
            (*step, *(downs[i] for i in offsets), *terms),
            after=after,
        )

    both, single = shape((2 * rows, width), F32), shape((2 * rows, width), BF16)
    (here,) = planned(raised((0, 1), blocks[:1]))
    (corner,) = planned(raised((0, 1), blocks[3:], (), here[2:3]))
    there = planned(*(raised((i,), blocks[1:3], here[-1:] * i, corner[:3] * (1 - i)) for i in (0, 1)))
    diagonal = lowered((0, 1), corner, single)
    first = lowered((0,), there[0], shape((4 * rows, width), F32), after=(diagonal,))
    sends = lowered((1,), there[1], (single,) * 2, first)
    own = lowered((0, 1), here, both, swap(diagonal, 6), after=sends[:1])
    back = [swap(s, 2 * k) for k, s in enumerate(sends, 1)]
    mine, theirs = call(
        functools.partial(half_kernel, rows),
        (shape((rows, width), F32), shape((rows, width), BF16)),
        (own, *back),
    )
    return call(last_kernel, shape((rows, width), BF16), (mine, swap(theirs, 2 * near)))


def exchanged(tokens, expert_ids, gate_weights, up_weight, down_weight, capacity):
    n_peers = lax.axis_size("ep")
    tok_rows, top_count = expert_ids.shape
    width_part = tokens.shape[1]
    flat_ids = expert_ids.reshape(-1)
    onehot = (flat_ids[:, None] == jnp.arange(n_peers, dtype=jnp.int32)[None, :]).astype(jnp.int32)
    before = jnp.cumsum(onehot, axis=0) - onehot
    ranking = jnp.sum(before * onehot, axis=1)
    slot_index = flat_ids * capacity + ranking
    token_of_row = jnp.arange(tok_rows * top_count, dtype=jnp.int32) // top_count
    outbound = (
        jnp.zeros((n_peers * capacity, width_part), tokens.dtype)
        .at[slot_index]
        .set(tokens[token_of_row])
    )
    inbound = lax.all_to_all(outbound, "ep", split_axis=0, concat_axis=0, tiled=True)
    pre_share = lax.psum_scatter(
        jnp.dot(inbound, up_weight[0], preferred_element_type=F32).astype(BF16),
        "rep",
        scatter_dimension=0,
        tiled=True,
    ).astype(F32)
    hidden_share = jax.nn.silu(pre_share).astype(BF16)
    expert_out = jnp.dot(
        lax.all_gather(hidden_share, "rep", axis=0, tiled=True),
        down_weight[0],
        preferred_element_type=F32,
    ).astype(BF16)
    returned = lax.all_to_all(expert_out, "ep", split_axis=0, concat_axis=0, tiled=True)
    picked = returned[slot_index].astype(F32).reshape(tok_rows, top_count, width_part)
    mixture = jnp.sum(gate_weights[:, :, None] * picked, axis=1)
    return mixture.astype(BF16)


def local(tokens, expert_ids, gate_weights, up_weight, down_weight):
    n = lax.axis_size("ep")
    rows, top = expert_ids.shape
    cap = min(rows, max(2, 3 * rows * top // (2 * n)))
    fits = n <= rows and 4 * rows <= LANES and n // 2 * rows == LANES and n & (n - 1) == 0
    plan = gathered if fits and lax.axis_size("rep") == 2 else exchanged
    return plan(tokens, expert_ids, gate_weights, up_weight, down_weight, cap)


def solution(mesh):
    placed = (
        P("ep", "rep"),
        P("ep", None),
        P("ep", None),
        P("ep", "rep", None),
        P("ep", None, "rep"),
    )
    return jax.shard_map(
        local, mesh=mesh, in_specs=placed, out_specs=P("ep", "rep"), check_vma=False
    )
```

```python
import functools

import jax
import jax.numpy as jnp
from jax import lax
from jax.experimental import pallas as pl
from jax.experimental.pallas import tpu as pltpu
from jax.sharding import PartitionSpec as P

LANES = 128
VMEM = pl.BlockSpec(memory_space=pltpu.VMEM)
HBM = pl.BlockSpec(memory_space=pltpu.HBM)
SMEM = pl.BlockSpec(memory_space=pltpu.SMEM)
F32, BF16 = jnp.float32, jnp.bfloat16


def call(kernel, outs, args, specs=None, scratch=(), limit=8 << 20, after=(), aliases={}):
    specs = specs or [VMEM] * len(args)
    args = [pltpu.with_memory_space_constraint(a, pltpu.HBM) if s is HBM else a for a, s in zip(args, specs)]

    def body(*refs):
        kernel(*refs[: len(args)], *refs[len(args) + len(after) :])

    return pl.pallas_call(
        body,
        out_shape=outs,
        in_specs=specs + [pl.BlockSpec(memory_space=pl.ANY)] * len(after),
        out_specs=jax.tree.map(lambda _: VMEM, outs),
        scratch_shapes=scratch,
        input_output_aliases=aliases,
        cost_estimate=pl.CostEstimate(flops=1, bytes_accessed=1, transcendentals=0),
        compiler_params=pltpu.CompilerParams(vmem_limit_bytes=limit),
    )(*args, *after)


def tie(x, *after):
    return call(lambda x_ref, out_ref: None, jax.ShapeDtypeStruct(x.shape, x.dtype), (x,), after=after, aliases={0: 0})


def iota(shape, dim):
    return lax.broadcasted_iota(jnp.int32, shape, dim)


def dot(a, b):
    return jnp.dot(a, b, preferred_element_type=F32)


def pack_kernel(tok_ref, ids_hbm, gates_hbm, out_ref, ids_ref, gates_ref, sems):
    rows, width = tok_ref.shape
    top = ids_ref.shape[0]
    copies = [
        pltpu.make_async_copy(ids_hbm, ids_ref, sems.at[0]),
        pltpu.make_async_copy(gates_hbm, gates_ref, sems.at[1]),
        pltpu.make_async_copy(tok_ref, out_ref.at[:, :width], sems.at[2]),
    ]
    for copy in copies:
        copy.start()
    copies[0].wait()
    copies[1].wait()
    gates = gates_ref[...]
    hi = gates.astype(BF16).astype(F32)
    mid = (gates - hi).astype(BF16).astype(F32)
    low = gates - hi - mid
    terms = jnp.concatenate([ids_ref[...].astype(F32), hi, mid, low], axis=0).astype(BF16)
    tiles = dot(terms, (iota((rows, LANES), 0) == iota((rows, LANES), 1) % rows).astype(BF16))
    ids, hi, mid, low = (tiles[i * top : (i + 1) * top] for i in range(4))
    group = iota((1, LANES), 1) // rows
    value = jnp.where(group == 0, hi, jnp.where(group == 1, mid, low))
    expert = iota((rows, LANES), 0).astype(F32)
    gate = jnp.zeros((rows, LANES), F32)
    mask = jnp.zeros((rows, LANES), F32)
    for k in range(top):
        hit = ids[k : k + 1, :] == expert
        gate = gate + jnp.where(hit, value[k : k + 1, :], 0.0)
        mask = mask + jnp.where(hit, 1.0, 0.0)
    before, after = iota((LANES, LANES), 0), iota((LANES, LANES), 1)
    earlier = ((before // rows == after // rows) & (before < after)).astype(BF16)
    rank = mask * (dot(mask.astype(BF16), earlier) + 1.0)
    routing = jnp.where(group < 3, gate, jnp.where(group == 3, rank, 0.0))
    out_ref[:, width:] = routing.astype(BF16)
    copies[2].wait()


def load_kernel(w_hbm, w_ref, sems):
    parts = sems.shape[0]
    rows = w_ref.shape[0] // parts
    copies = [
        pltpu.make_async_copy(w_hbm.at[pl.ds(i * rows, rows)], w_ref.at[pl.ds(i * rows, rows)], sems.at[i])
        for i in range(parts)
    ]
    for copy in copies:
        copy.start()
    for copy in copies:
        copy.wait()


def join_kernel(a_ref, b_ref, out_ref):
    rows = a_ref.shape[0]
    out_ref[:rows, :] = a_ref[...]
    out_ref[rows:, :] = b_ref[...]


def routed(routing, rows, q):
    n = routing.shape[0]
    first = pltpu.roll(routing, LANES - q * rows, 1) if q else routing
    lined = pltpu.roll(first, 0, 1, stride=rows, stride_axis=0)
    mine = iota((n, LANES), 1) // rows == iota((n, LANES), 0)
    return jnp.sum(jnp.where(mine, lined, 0.0), axis=0, keepdims=True)


def slot_of(routing, rows, cap):
    rank = routed(routing, rows, 3).astype(jnp.int32)
    return jnp.where(rank > 0, iota((1, LANES), 1) // rows * cap + rank - 1, -1)


def selection(routing, rows, cap):
    hit = iota((LANES // rows * cap, LANES), 0) == slot_of(routing, rows, cap)
    return jnp.where(hit, 1.0, 0.0)


def up_kernel(rows, cap, offsets, *refs):
    weights, blocks, (pre_ref, routing_ref, x_ref) = refs[: len(offsets)], refs[len(offsets) : -3], refs[-3:]
    width = weights[0].shape[0]
    pieces = []
    for i, ref in enumerate(blocks):
        size = ref.shape[0]
        x_ref[i * size : (i + 1) * size, :] = ref[:, :width]
        pieces += [ref[j : j + rows, width:].astype(F32) for j in range(0, size, rows)]
    tokens = len(pieces) * rows
    x_ref[tokens:, :] = jnp.zeros((LANES - tokens, width), BF16)
    lines = []
    for offset in offsets:
        here = iota((rows, LANES), 0) == lax.axis_index("ep") ^ offset
        lines += [jnp.sum(jnp.where(here, piece, 0.0), axis=0, keepdims=True) for piece in pieces]
    routing = jnp.concatenate(lines + [jnp.zeros_like(lines[0])] * (LANES // rows - len(lines)), axis=0)
    routing_ref[...] = routing
    step = 256
    parts = []
    for c in range(0, weights[0].shape[1], step):
        parts.append([dot(x_ref[...], w_ref[:, c : c + step])[:tokens].astype(BF16) for w_ref in weights])
    sel = selection(routing, rows, cap)[: len(lines) * cap, : len(lines) * rows].astype(BF16)
    for i, part in enumerate(parts):
        pre_ref[:, i * step : (i + 1) * step] = dot(sel, jnp.concatenate(part, axis=0)).astype(BF16)


def plan_kernel(rows, cap, *refs):
    count = len(refs) // 3
    for routing_ref, turned_ref, gate_ref in zip(refs[:count], refs[count::2], refs[count + 1 :: 2]):
        routing = routing_ref[...]
        tokens, slots = turned_ref.shape
        turned_ref[...] = jnp.transpose(selection(routing, rows, cap))[:tokens, :slots].astype(BF16)
        gate = routed(routing, rows, 0) + routed(routing, rows, 1) + routed(routing, rows, 2)
        gate_ref[...] = jnp.transpose(jnp.broadcast_to(gate, (LANES, LANES)))[:tokens]


def down_kernel(experts, terms, turned_ref, gate_ref, a_ref, b_ref, *refs):
    weights, sums, outs = refs[:experts], refs[experts : experts + terms], refs[experts + terms :]
    v = a_ref[...].astype(F32) + b_ref[...].astype(F32)
    hidden = (v / (1.0 + jnp.exp(-v))).astype(BF16)
    hidden = dot(turned_ref[...], hidden).astype(BF16)
    size = hidden.shape[0] // experts
    rows = outs[0].shape[0]
    step = 256
    for c in range(0, weights[0].shape[1], step):
        total = [ref[:, c : c + step].astype(F32) for ref in sums]
        for i, w_ref in enumerate(weights):
            at = slice(i * size, (i + 1) * size)
            out = dot(hidden[at], w_ref[:, c : c + step]).astype(BF16).astype(F32)
            total.append(out * jnp.concatenate([gate_ref[at, :]] * (step // LANES), axis=1))
        total = sum(total[1:], total[0])
        for k, ref in enumerate(outs):
            ref[:, c : c + step] = total[k * rows : (k + 1) * rows].astype(ref.dtype)


def half_kernel(rows, own_ref, *refs):
    total = own_ref[...]
    for ref in refs[:-2]:
        total = total + ref[...].astype(F32)
    keep_ref, send_ref = refs[-2:]
    keep_ref[...] = total[:rows]
    send_ref[...] = total[rows:].astype(BF16)


def last_kernel(keep_ref, got_ref, out_ref):
    out_ref[...] = (keep_ref[...] + got_ref[...].astype(F32)).astype(BF16)


def gathered(tokens, expert_ids, gate_weights, up_weight, down_weight, cap):
    n = lax.axis_size("ep")
    rows, width = tokens.shape
    near = n // 4
    hidden = up_weight.shape[2]
    shape = jax.ShapeDtypeStruct
    dma = pltpu.SemaphoreType.DMA

    def swap(x, distance):
        return lax.ppermute(x, "ep", [(i, i ^ distance) for i in range(n)])

    def load(weight, *after):
        out = pltpu.VMEM(weight.shape, BF16)
        return call(load_kernel, out, (weight,), specs=[HBM], scratch=[dma((8,))], after=after)

    packed = call(
        pack_kernel,
        shape((rows, width + LANES), BF16),
        (tokens, expert_ids.T, gate_weights.T),
        specs=[HBM] * 3,
        scratch=[pltpu.VMEM(expert_ids.shape[::-1], jnp.int32), pltpu.VMEM(expert_ids.shape[::-1], F32), dma((3,))],
    )
    up = load(up_weight[0])
    far = swap(packed, 2 * near)
    block = call(join_kernel, shape((2 * rows, width + LANES), BF16), (packed, far), after=(up,))
    blocks = [block] + [swap(block, 2 * k) for k in range(1, near)]
    down = down_weight[0]
    ups, downs = (up, swap(up_weight[0], 1)), (down, swap(down, 1))

    def raised(offsets, blocks, before=(), after=()):
        count = len(offsets) * 2 * len(blocks)
        pre, routing = call(
            functools.partial(up_kernel, rows, cap, offsets),
            (shape((count * cap, hidden), BF16), shape((LANES // rows, LANES), F32)),
            (*(ups[i] for i in offsets), *blocks),
            scratch=[pltpu.VMEM((LANES, width), BF16)],
            after=after,
        )
        if before:
            pre = tie(pre, *before)
        return count, routing, pre, lax.ppermute(pre, "rep", [(0, 1), (1, 0)])

    def planned(*steps):
        outs = []
        for count, *_ in steps:
            outs += [shape((count * rows, count * cap), BF16), shape((count * rows, LANES), F32)]
        made = call(functools.partial(plan_kernel, rows, cap), tuple(outs), tuple(step[1] for step in steps))
        return [(*made[2 * i : 2 * i + 2], *step[2:]) for i, step in enumerate(steps)]

    def lowered(offsets, step, outs, *terms, after=()):
        return call(
            functools.partial(down_kernel, len(offsets), len(terms)),
            outs,
            (*step, *(downs[i] for i in offsets), *terms),
            after=after,
        )

    both, single = shape((2 * rows, width), F32), shape((2 * rows, width), BF16)
    (here,) = planned(raised((0, 1), blocks[:1]))
    (corner,) = planned(raised((0, 1), blocks[3:], (), here[2:3]))
    there = planned(*(raised((i,), blocks[1:3], here[-1:] * i, corner[:3] * (1 - i)) for i in (0, 1)))
    diagonal = lowered((0, 1), corner, single)
    first = lowered((0,), there[0], shape((4 * rows, width), F32), after=(diagonal,))
    sends = lowered((1,), there[1], (single,) * 2, first)
    own = lowered((0, 1), here, both, swap(diagonal, 6), after=sends[:1])
    back = [swap(s, 2 * k) for k, s in enumerate(sends, 1)]
    mine, theirs = call(
        functools.partial(half_kernel, rows),
        (shape((rows, width), F32), shape((rows, width), BF16)),
        (own, *back),
    )
    return call(last_kernel, shape((rows, width), BF16), (mine, swap(theirs, 2 * near)))


def exchanged(tokens, expert_ids, gate_weights, up_weight, down_weight, capacity):
    n_peers = lax.axis_size("ep")
    tok_rows, top_count = expert_ids.shape
    width_part = tokens.shape[1]
    flat_ids = expert_ids.reshape(-1)
    onehot = (flat_ids[:, None] == jnp.arange(n_peers, dtype=jnp.int32)[None, :]).astype(jnp.int32)
    before = jnp.cumsum(onehot, axis=0) - onehot
    ranking = jnp.sum(before * onehot, axis=1)
    slot_index = flat_ids * capacity + ranking
    token_of_row = jnp.arange(tok_rows * top_count, dtype=jnp.int32) // top_count
    outbound = (
        jnp.zeros((n_peers * capacity, width_part), tokens.dtype)
        .at[slot_index]
        .set(tokens[token_of_row])
    )
    inbound = lax.all_to_all(outbound, "ep", split_axis=0, concat_axis=0, tiled=True)
    pre_share = lax.psum_scatter(
        jnp.dot(inbound, up_weight[0], preferred_element_type=F32).astype(BF16),
        "rep",
        scatter_dimension=0,
        tiled=True,
    ).astype(F32)
    hidden_share = jax.nn.silu(pre_share).astype(BF16)
    expert_out = jnp.dot(
        lax.all_gather(hidden_share, "rep", axis=0, tiled=True),
        down_weight[0],
        preferred_element_type=F32,
    ).astype(BF16)
    returned = lax.all_to_all(expert_out, "ep", split_axis=0, concat_axis=0, tiled=True)
    picked = returned[slot_index].astype(F32).reshape(tok_rows, top_count, width_part)
    mixture = jnp.sum(gate_weights[:, :, None] * picked, axis=1)
    return mixture.astype(BF16)


def local(tokens, expert_ids, gate_weights, up_weight, down_weight):
    n = lax.axis_size("ep")
    rows, top = expert_ids.shape
    cap = min(rows, max(2, 3 * rows * top // (2 * n)))
    fits = n <= rows and 4 * rows <= LANES and n // 2 * rows == LANES and n & (n - 1) == 0
    plan = gathered if fits and lax.axis_size("rep") == 2 else exchanged
    return plan(tokens, expert_ids, gate_weights, up_weight, down_weight, cap)


def solution(mesh):
    placed = (
        P("ep", "rep"),
        P("ep", None),
        P("ep", None),
        P("ep", "rep", None),
        P("ep", None, "rep"),
    )
    return jax.shard_map(
        local, mesh=mesh, in_specs=placed, out_specs=P("ep", "rep"), check_vma=False
    )
```
